32 devices in a mesh: lists: 16 (over z, x, core), sub: 2 (over y).
Axes of the slice: x: 2, y: 2, z: 4, core: 2. Of those that a mesh axis runs over, the one named last changes fastest.
Arguments:
- vectors: bfloat16 [768, 6144], P('sub', 'lists'), may hold values from -6 to 6
- list_ids: int32 [6144], P('lists'), may hold values from 0 to 63
- counts: int32 [16, 16], replicated, may hold values from 0 to 24, as said below
- coarse: bfloat16 [768, 1024], P(None, ('lists', 'sub')), may hold values from -3 to 3
- codebook_init: float32 [768, 256], P('sub'), may hold values from -6 to 6
- codes: int32 [2, 96, 6144], P(None, 'sub', 'lists'), may hold values from 0 to 255
Outputs:
- codebook: float32 [768, 256], P('sub')
- leftover: bfloat16 [768, 6144], P('sub', 'lists')
The draws below stay inside these ranges and needn't reach their ends.
Inputs may be any that keep to these rules, and one draw needn't show every extreme that they name: `counts`: counts of used slots in each block; in every draw one owner receives full blocks of 24 from every sender. `list_ids`: every slot names one of its block owner's lists.
All inputs are finite; a program needn't handle non-finite values.
Results may differ from the reference program's by a relative error of at most 0.0051.
Values may be sent and summed in bfloat16 or wider, within the bound.
A program may use at most 64 MiB of HBM per device.

```python
import jax
import jax.numpy as jnp
from jax import lax

D = 768
M = 96
K = 256
DS = 8
LISTS_DEV = 64
NLIST = 1024
CAP = 24
ITERS = 2
ROWS_DEV = 384
SLOTS = 6144
N_LISTS = 16


def draw_counts(key, part):
    owners = ROWS_DEV // CAP
    first, second, third = jax.random.split(key, 3)
    base = jax.random.randint(first, (owners, owners), 0, CAP + 1)
    levels = jax.random.randint(second, (1, owners), 2, 5)
    scaled = jnp.minimum(CAP, base * levels // 3)
    hottest = jax.random.randint(third, (), 0, owners)
    column = jnp.arange(owners, dtype=jnp.int32)[None, :]
    return jnp.where(column == hottest, CAP, scaled).astype(jnp.int32)


def touch_ends(values, own_key, least, high):
    place = [jax.random.randint(jax.random.fold_in(own_key, axis), (), 0, length) for axis, length in enumerate(values.shape)]
    main_axis = values.shape.index(max(values.shape))
    neighbour = place[:main_axis] + [(place[main_axis] + 1) % values.shape[main_axis]] + place[main_axis + 1:]
    return values.at[tuple(place)].set(least).at[tuple(neighbour)].set(high)


def shard_levels(key, extent, shards, smallest, high):
    def one(axis_at, parts):
        steps = jax.random.uniform(jax.random.fold_in(jax.random.fold_in(key, 6), axis_at), (parts,), jnp.float32, smallest / len(shards), high / len(shards))
        return jnp.repeat(jnp.exp(steps), extent[axis_at] // parts).reshape((-1,) + (1,) * (len(extent) - axis_at - 1))

    factor_of = one(*shards[0])
    for cut in shards[1:]:
        factor_of = factor_of * one(*cut)
    return factor_of


def bell_draw(rng, dims, scale, bound, cuts=(), kind=jnp.bfloat16):
    gain = shard_levels(rng, dims, cuts, -0.22, 0.18) if cuts else 1.0
    values = jax.random.normal(rng, dims, jnp.float32) * scale * gain
    return jnp.minimum(jnp.maximum(values, -bound), bound).astype(kind)


def setup_inputs(seed: int = 0) -> dict:
    arg_keys = jax.random.split(jax.random.key(seed), 7)
    return {
        "vectors": bell_draw(arg_keys[0], (D, SLOTS), 1.0, 6.0, ((0, 2), (1, 16))),
        "list_ids": touch_ends(jax.random.randint(arg_keys[1], (SLOTS,), 0, LISTS_DEV), jax.random.fold_in(arg_keys[1], 1), 0, LISTS_DEV - 1).astype(jnp.int32),
        "counts": draw_counts(jax.random.fold_in(arg_keys[6], 71), 0),
        "coarse": bell_draw(arg_keys[3], (D, NLIST), 0.5, 3.0, ((1, 32),)),
        "codebook_init": bell_draw(arg_keys[4], (D, K), 1.0, 6.0, ((0, 2),), jnp.float32),
        "codes": touch_ends(jax.random.randint(arg_keys[5], (ITERS, M, SLOTS), 0, K), jax.random.fold_in(arg_keys[5], 1), 0, K - 1).astype(jnp.int32),
    }


def owner_residual(vectors, list_ids, counts, coarse, owner):
    blocks = lax.dynamic_index_in_dim(vectors.reshape(D, N_LISTS, N_LISTS, CAP), owner, 2, keepdims=False)
    blocks = blocks.reshape(D, ROWS_DEV)
    labels = lax.dynamic_index_in_dim(list_ids.reshape(N_LISTS, N_LISTS, CAP), owner, 1, keepdims=False)
    global_list = (owner * LISTS_DEV + labels.reshape(ROWS_DEV)).astype(jnp.int32)
    centre = jnp.take(coarse, global_list, axis=1).astype(jnp.float32)
    residual = (blocks.astype(jnp.float32) - centre).astype(jnp.bfloat16)
    block_counts = lax.dynamic_index_in_dim(counts, owner, 1, keepdims=False)
    valid = (jnp.arange(CAP, dtype=jnp.int32)[None, :] < block_counts[:, None]).reshape(ROWS_DEV)
    return residual, valid


def reference(vectors, list_ids, counts, coarse, codebook_init, codes):
    offsets = (jnp.arange(M, dtype=jnp.int32) * K)[:, None]

    def gather_sums(owner):
        residual, valid = owner_residual(vectors, list_ids, counts, coarse, owner)
        mask = valid.astype(jnp.float32)
        own_codes = lax.dynamic_slice_in_dim(codes, (owner * ROWS_DEV).astype(jnp.int32), ROWS_DEV, 2)
        values = residual.astype(jnp.float32).reshape(M, DS, ROWS_DEV) * mask[None, None, :]
        values = jnp.transpose(values, (0, 2, 1)).reshape(M * ROWS_DEV, DS)
        weights = jnp.broadcast_to(mask[None, :], (M, ROWS_DEV)).reshape(M * ROWS_DEV)
        sums_list = []
        count_list = []
        for iteration in range(ITERS):
            labels = (own_codes[iteration] + offsets).reshape(M * ROWS_DEV)
            total = jax.ops.segment_sum(values, labels, num_segments=M * K)
            sums_list.append(jnp.transpose(total.reshape(M, K, DS), (0, 2, 1)).reshape(D, K))
            count_list.append(jax.ops.segment_sum(weights, labels, num_segments=M * K).reshape(M, K))
        return jnp.stack(sums_list), jnp.stack(count_list)

    all_sums, all_counts = lax.map(gather_sums, jnp.arange(N_LISTS, dtype=jnp.int32))
    sums = jnp.sum(all_sums, axis=0)
    number = jnp.sum(all_counts, axis=0)
    weight = 0.25 * jnp.sum(counts).astype(jnp.float32) / K
    codebook = codebook_init
    for iteration in range(ITERS):
        spread = jnp.repeat(number[iteration], DS, axis=0)
        codebook = (sums[iteration] + weight * codebook) / (spread + weight)
    split_book = codebook.reshape(M, DS, K)

    def gather_left(owner):
        residual, valid = owner_residual(vectors, list_ids, counts, coarse, owner)
        own_codes = lax.dynamic_slice_in_dim(codes[ITERS - 1], (owner * ROWS_DEV).astype(jnp.int32), ROWS_DEV, 1)
        picked = jnp.take_along_axis(split_book, own_codes[:, None, :], axis=2).reshape(D, ROWS_DEV)
        left = jnp.where(valid[None, :], residual.astype(jnp.float32) - picked, 0.0)
        return left.astype(jnp.bfloat16)

    stacked = lax.map(gather_left, jnp.arange(N_LISTS, dtype=jnp.int32))
    leftover = jnp.transpose(stacked, (1, 0, 2)).reshape(D, N_LISTS * ROWS_DEV)
    return codebook, leftover
```

```python
import jax
import jax.numpy as jnp
from jax import lax
from jax.sharding import PartitionSpec as P

K = 256
DS = 8
LISTS_DEV = 64
ITERS = 2


def shards(vectors, list_ids, counts, coarse, codebook_init, codes):
    features, rows = vectors.shape
    owners = lax.axis_size("lists")
    owner = lax.axis_index("lists")
    block = rows // owners
    subspaces = features // DS
    mine = lax.all_to_all(coarse, "sub", split_axis=0, concat_axis=1, tiled=True)
    list_iota = jnp.arange(LISTS_DEV, dtype=jnp.int32)
    arrived = lax.all_to_all(vectors, "lists", split_axis=1, concat_axis=1, tiled=True)
    labels = lax.all_to_all(
        list_ids.reshape(1, rows), "lists", split_axis=1, concat_axis=1, tiled=True
    ).reshape(rows)
    selector = (labels[None, :] == list_iota[:, None]).astype(jnp.bfloat16)
    centre = jnp.dot(mine, selector, preferred_element_type=jnp.float32)
    residual = (arrived.astype(jnp.float32) - centre).astype(jnp.bfloat16)
    block_counts = lax.dynamic_index_in_dim(counts, owner, 1, keepdims=False)
    valid = (jnp.arange(block, dtype=jnp.int32)[None, :] < block_counts[:, None]).reshape(rows)
    code_iota = jnp.arange(K, dtype=jnp.int32)
    split_res = residual.reshape(subspaces, DS, rows)
    group_size = 4
    groups = subspaces // group_size
    grouped_res = split_res.reshape(groups, group_size, DS, rows)
    grouped_codes = jnp.swapaxes(codes, 0, 1).reshape(groups, group_size, ITERS, rows)

    def group_sums(packed):
        sub_res, sub_codes = packed
        one_hot = (sub_codes[:, :, None, :] == code_iota[None, None, :, None]) & valid[
            None, None, None, :
        ]
        one_hot = one_hot.astype(jnp.bfloat16)
        sums = jnp.einsum("gdr,gtkr->tgdk", sub_res, one_hot, preferred_element_type=jnp.float32)
        tally = jnp.swapaxes(jnp.sum(one_hot, axis=3, dtype=jnp.float32), 0, 1)
        return (sums, tally)

    part_sums, part_counts = lax.map(group_sums, (grouped_res, grouped_codes))
    part_sums = jnp.swapaxes(part_sums, 0, 1).reshape(ITERS, features, K)
    part_counts = jnp.swapaxes(part_counts, 0, 1).reshape(ITERS, subspaces, K)
    weight = 0.25 * jnp.sum(counts).astype(jnp.float32) / K
    total_sums, total_counts = lax.psum((part_sums, part_counts), "lists")
    codebook = codebook_init
    for iteration in range(ITERS):
        spread = jnp.repeat(total_counts[iteration], DS, axis=0)
        codebook = (total_sums[iteration] + weight * codebook) / (spread + weight)
    high = codebook.astype(jnp.bfloat16)
    low = (codebook - high.astype(jnp.float32)).astype(jnp.bfloat16)
    books = jnp.concatenate(
        [high.reshape(subspaces, DS, K), low.reshape(subspaces, DS, K)], axis=1
    ).reshape(groups, group_size, 2 * DS, K)

    def group_pick(packed):
        book, sub_codes = packed
        one_hot = (sub_codes[:, None, :] == code_iota[None, :, None]).astype(jnp.bfloat16)
        both = jnp.einsum("gdk,gkr->gdr", book, one_hot, preferred_element_type=jnp.float32)
        return both[:, :DS] + both[:, DS:]

    picked = lax.map(group_pick, (books, grouped_codes[:, :, ITERS - 1]))
    picked = picked.reshape(subspaces, DS, rows)
    leftover = jnp.where(valid[None, None, :], split_res.astype(jnp.float32) - picked, 0.0)
    leftover = leftover.astype(jnp.bfloat16).reshape(features, rows)
    return (codebook, leftover)


def solution(mesh):
    return jax.shard_map(
        shards,
        mesh=mesh,
        in_specs=(
            P("sub", "lists"),
            P("lists"),
            P(),
            P(None, ("lists", "sub")),
            P("sub", None),
            P(None, "sub", "lists"),
        ),
        out_specs=(P("sub", None), P("sub", "lists")),
        check_vma=False,
    )
```

```python
import functools

import jax
import jax.numpy as jnp
from jax import lax
from jax.experimental import pallas as pl
from jax.experimental.pallas import tpu as pltpu
from jax.sharding import PartitionSpec as P

K = 256
DS = 8
LISTS_DEV = 64
ITERS = 2


def shards(vectors, list_ids, counts, coarse, codebook_init, codes):
    features, rows = vectors.shape
    owners = lax.axis_size("lists")
    owner = lax.axis_index("lists")
    block = rows // owners
    subspaces = features // DS
    mine = lax.all_to_all(coarse, "sub", split_axis=0, concat_axis=1, tiled=True)
    list_iota = jnp.arange(LISTS_DEV, dtype=jnp.int32)
    arrived = lax.all_to_all(vectors, "lists", split_axis=1, concat_axis=1, tiled=True)
    labels = lax.all_to_all(
        list_ids.reshape(1, rows), "lists", split_axis=1, concat_axis=1, tiled=True
    ).reshape(rows)
    selector = (labels[None, :] == list_iota[:, None]).astype(jnp.bfloat16)
    centre = jnp.dot(mine, selector, preferred_element_type=jnp.float32)
    residual = (arrived.astype(jnp.float32) - centre).astype(jnp.bfloat16)
    block_counts = lax.dynamic_index_in_dim(counts, owner, 1, keepdims=False)
    valid = (jnp.arange(block, dtype=jnp.int32)[None, :] < block_counts[:, None]).reshape(rows)
    code_iota = jnp.arange(K, dtype=jnp.int32)
    split_res = residual.reshape(subspaces, DS, rows)
    group_size = 4
    groups = subspaces // group_size
    grouped_res = split_res.reshape(groups, group_size, DS, rows)
    grouped_codes = jnp.swapaxes(codes, 0, 1).reshape(groups, group_size, ITERS, rows)

    def group_sums(packed):
        sub_res, sub_codes = packed
        one_hot = (sub_codes[:, :, None, :] == code_iota[None, None, :, None]) & valid[
            None, None, None, :
        ]
        one_hot = one_hot.astype(jnp.bfloat16)
        sums = jnp.einsum("gdr,gtkr->tgdk", sub_res, one_hot, preferred_element_type=jnp.float32)
        tally = jnp.swapaxes(jnp.sum(one_hot, axis=3, dtype=jnp.float32), 0, 1)
        return (sums, tally)

    part_sums, part_counts = lax.map(group_sums, (grouped_res, grouped_codes))
    part_sums = jnp.swapaxes(part_sums, 0, 1).reshape(ITERS, features, K)
    part_counts = jnp.swapaxes(part_counts, 0, 1).reshape(ITERS, subspaces, K)
    weight = 0.25 * jnp.sum(counts).astype(jnp.float32) / K
    total_sums, total_counts = lax.psum((part_sums, part_counts), "lists")
    codebook = codebook_init
    for iteration in range(ITERS):
        spread = jnp.repeat(total_counts[iteration], DS, axis=0)
        codebook = (total_sums[iteration] + weight * codebook) / (spread + weight)
    high = codebook.astype(jnp.bfloat16)
    low = (codebook - high.astype(jnp.float32)).astype(jnp.bfloat16)
    books = jnp.concatenate(
        [high.reshape(subspaces, DS, K), low.reshape(subspaces, DS, K)], axis=1
    ).reshape(groups, group_size, 2 * DS, K)

    def group_pick(packed):
        book, sub_codes = packed
        one_hot = (sub_codes[:, None, :] == code_iota[None, :, None]).astype(jnp.bfloat16)
        both = jnp.einsum("gdk,gkr->gdr", book, one_hot, preferred_element_type=jnp.float32)
        return both[:, :DS] + both[:, DS:]

    picked = lax.map(group_pick, (books, grouped_codes[:, :, ITERS - 1]))
    picked = picked.reshape(subspaces, DS, rows)
    leftover = jnp.where(valid[None, None, :], split_res.astype(jnp.float32) - picked, 0.0)
    leftover = leftover.astype(jnp.bfloat16).reshape(features, rows)
    return (codebook, leftover)


def remote(src, dst, send_sem, recv_sem, device):
    return pltpu.make_async_remote_copy(
        src_ref=src,
        dst_ref=dst,
        send_sem=send_sem,
        recv_sem=recv_sem,
        device_id=device,
        device_id_type=pl.DeviceIdType.MESH,
    )


def kernel(
    owners, subs, vec, coarse, mask, weight, init, codes,
    book_out, left_out,
    arrived, centres, res, parts_out, parts_in, total, books,
    vec_send, vec_recv, cen_send, cen_recv, part_send, part_recv, book_send, book_recv,
):
    me = lax.axis_index("lists")
    my_sub = lax.axis_index("sub")
    features, rows = res.shape
    cap = vec.shape[1] // 2
    pieces = features // DS // owners
    height = pieces * DS

    def after(d):
        return lax.rem(me + d, owners)

    def before(d):
        return lax.rem(me + owners - d, owners)

    def sub_after(d):
        return lax.rem(my_sub + d, subs)

    barrier = pltpu.get_barrier_semaphore()

    @pl.loop(1, owners)
    def _(d):
        pl.semaphore_signal(
            barrier, inc=1, device_id={"lists": after(d)}, device_id_type=pl.DeviceIdType.MESH
        )

    for d in range(1, subs):
        pl.semaphore_signal(
            barrier, inc=1, device_id={"sub": sub_after(d)}, device_id_type=pl.DeviceIdType.MESH
        )
    pl.semaphore_wait(barrier, owners - 1 + subs - 1)

    def cen_copy(q, slot):
        return remote(
            coarse.at[q], centres.at[slot], cen_send.at[q], cen_recv.at[slot], {"sub": q}
        )

    def vec_copy(p, slot):
        return remote(
            vec.at[p], arrived.at[slot], vec_send.at[p], vec_recv.at[slot], {"lists": p}
        )

    def part_copy(p, slot):
        return remote(
            parts_out.at[p], parts_in.at[slot], part_send.at[p], part_recv.at[slot], {"lists": p}
        )

    def book_copy(p, slot):
        return remote(
            books.at[me], books.at[slot], book_send.at[p], book_recv.at[slot], {"lists": p}
        )

    for d in range(1, subs):
        cen_copy(sub_after(d), my_sub).start()

    @pl.loop(1, owners)
    def _(d):
        vec_copy(after(d), me).start()

    arrived[me] = vec[me]
    centres[my_sub] = coarse[my_sub]
    for d in range(1, subs):
        q = sub_after(d)
        cen_copy(q, q).wait_recv()

    @pl.loop(1, owners)
    def _(d):
        p = before(d)
        vec_copy(p, p).wait_recv()

    half = vec.shape[2]
    slab = arrived[...].astype(jnp.float32)
    full = jnp.concatenate(
        [slab[:, :cap].reshape(rows, half), slab[:, cap:].reshape(rows, half)], axis=1
    )
    labels = full[:, features:]
    lanes = lax.broadcasted_iota(jnp.int32, labels.shape, 1).astype(jnp.float32)
    selector = (labels == lanes).astype(jnp.float32).astype(jnp.bfloat16)
    lists = centres[...].reshape(subs * centres.shape[1], features)
    lists = jnp.concatenate(
        [lists, jnp.zeros((labels.shape[1] - lists.shape[0], features), lists.dtype)], axis=0
    )
    centre = jnp.dot(selector, lists, preferred_element_type=jnp.float32)
    residual = (full[:, :features] - centre).astype(jnp.bfloat16).astype(jnp.float32)
    used = mask[...]
    res[...] = jnp.where(used > 0.0, residual.T, 0.0)

    def one_hot(t, m):
        code = codes[t, pl.ds(m, 1), :]
        iota = lax.broadcasted_iota(jnp.int32, (K, rows), 0)
        return (code == iota).astype(jnp.float32).astype(jnp.bfloat16)

    def rows_of(m):
        return pl.ds(pl.multiple_of(m * DS, DS), DS)

    def part(p, t):
        sums = []
        tally = jnp.zeros((DS, K), jnp.float32)
        line = lax.broadcasted_iota(jnp.int32, (DS, K), 0)
        for j in range(pieces):
            m = p * pieces + j
            left = jnp.concatenate(
                [res[rows_of(m), :], jnp.broadcast_to(used, (DS, rows))], axis=0
            ).astype(jnp.bfloat16)
            both = lax.dot_general(
                left, one_hot(t, m), (((1,), (1,)), ((), ())),
                preferred_element_type=jnp.float32,
            )
            sums.append(both[:DS])
            number = both[DS:]
            coarse_part = jnp.floor(number * (1.0 / 128.0)) * 128.0
            tally = jnp.where(line == j, coarse_part, tally)
            tally = jnp.where(line == pieces + j, number - coarse_part, tally)
        return jnp.concatenate(sums + [tally], axis=0)

    @pl.loop(1, owners)
    def _(d):
        p = after(d)
        for t in range(ITERS):
            parts_out[p, t] = part(p, t).astype(jnp.bfloat16)
        part_copy(p, me).start()

    for t in range(ITERS):
        total[t] = part(me, t)

    @pl.loop(1, owners)
    def _(d):
        p = before(d)
        part_copy(p, p).wait_recv()
        for t in range(ITERS):
            total[t] += parts_in[p, t].astype(jnp.float32)

    scale = weight[...]
    mine = []
    for j in range(pieces):
        book = init[rows_of(me * pieces + j), :]
        for t in range(ITERS):
            number = (
                total[t, height + j : height + j + 1]
                + total[t, height + pieces + j : height + pieces + j + 1]
            )
            book = (total[t, j * DS : (j + 1) * DS] + scale * book) / (number + scale)
        mine.append(book)
    mine = jnp.concatenate(mine, axis=0)
    books[me] = jnp.concatenate([mine[:, : K // 2], mine[:, K // 2 :]], axis=0).astype(
        jnp.bfloat16
    )

    @pl.loop(1, owners)
    def _(d):
        book_copy(after(d), me).start()

    def finish(p):
        pair = books[p].astype(jnp.float32)
        book = jnp.concatenate([pair[:height], pair[height:]], axis=1)
        for j in range(pieces):
            m = p * pieces + j
            own = book[j * DS : (j + 1) * DS]
            book_out[rows_of(m), :] = own
            picked = jnp.dot(
                own.astype(jnp.bfloat16), one_hot(ITERS - 1, m),
                preferred_element_type=jnp.float32,
            )
            res[rows_of(m), :] = jnp.where(used > 0.0, res[rows_of(m), :] - picked, 0.0)

    finish(me)

    @pl.loop(1, owners)
    def _(d):
        p = before(d)
        book_copy(p, p).wait_recv()
        finish(p)

    left_out[...] = res[...].astype(jnp.bfloat16)

    for d in range(1, subs):
        cen_copy(sub_after(d), my_sub).wait_send()

    @pl.loop(1, owners)
    def _(d):
        p = after(d)
        vec_copy(p, me).wait_send()
        part_copy(p, me).wait_send()
        book_copy(p, me).wait_send()


def fused(vectors, list_ids, counts, coarse, codebook_init, codes):
    features, rows = vectors.shape
    owners = lax.axis_size("lists")
    subs = lax.axis_size("sub")
    owner = lax.axis_index("lists")
    cap = rows // owners
    height = features // owners
    width = features + 128
    vec = jnp.concatenate(
        [
            vectors.T,
            jnp.broadcast_to(list_ids[:, None], (rows, 128)).astype(jnp.bfloat16),
        ],
        axis=1,
    )
    vec = vec.reshape(owners, cap, 2, width // 2).swapaxes(1, 2)
    vec = vec.reshape(owners, 2 * cap, width // 2)
    per = coarse.shape[1]
    slabs = coarse.reshape(subs, features, per).swapaxes(1, 2)
    block_counts = lax.dynamic_index_in_dim(counts, owner, 1, keepdims=False)
    mask = (jnp.arange(cap, dtype=jnp.int32)[None, :] < block_counts[:, None]).reshape(1, rows)
    mask = mask.astype(jnp.float32)
    weight = jnp.full((1, K), 0.25 * jnp.sum(counts).astype(jnp.float32) / K)
    vmem = pl.BlockSpec(memory_space=pltpu.VMEM)
    dma = pltpu.SemaphoreType.DMA
    part = (owners, ITERS, height + DS, K)
    return pl.pallas_call(
        functools.partial(kernel, owners, subs),
        out_shape=(
            jax.ShapeDtypeStruct((features, K), jnp.float32),
            jax.ShapeDtypeStruct((features, rows), jnp.bfloat16),
        ),
        in_specs=[vmem] * 6,
        out_specs=(vmem, vmem),
        scratch_shapes=[
            pltpu.VMEM(vec.shape, jnp.bfloat16),
            pltpu.VMEM(slabs.shape, jnp.bfloat16),
            pltpu.VMEM((features, rows), jnp.float32),
            pltpu.VMEM(part, jnp.bfloat16),
            pltpu.VMEM(part, jnp.bfloat16),
            pltpu.VMEM(part[1:], jnp.float32),
            pltpu.VMEM((owners, 2 * height, K // 2), jnp.bfloat16),
            dma((owners,)), dma((owners,)), dma((subs,)), dma((subs,)),
            dma((owners,)), dma((owners,)), dma((owners,)), dma((owners,)),
        ],
        compiler_params=pltpu.CompilerParams(
            collective_id=0, has_side_effects=True, vmem_limit_bytes=40 * 1024 * 1024
        ),
    )(vec, slabs, mask, weight, codebook_init, codes)


def fits(owners, subs, vectors, coarse):
    features = vectors.shape[0] // subs
    rows = vectors.shape[1] // owners
    spaces = features // DS
    per = coarse.shape[1] // (owners * subs)
    return (
        features % 256 == 128
        and spaces % owners == 0
        and 2 * (spaces // owners) <= DS
        and (features // owners + DS) % 16 == 0
        and (rows // owners) % DS == 0
        and per % 16 == 0
        and per * subs <= 128
    )


def dispatch(owners, subs, *args):
    whole_features = args[0].shape[0] * subs
    sizes = (
        jax.ShapeDtypeStruct((whole_features, args[0].shape[1] * owners), jnp.bfloat16),
        jax.ShapeDtypeStruct((whole_features, args[3].shape[1] * owners * subs), jnp.bfloat16),
    )
    return (fused if fits(owners, subs, *sizes) else shards)(*args)


def solution(mesh):
    return jax.shard_map(
        functools.partial(dispatch, mesh.shape["lists"], mesh.shape["sub"]),
        mesh=mesh,
        in_specs=(
            P("sub", "lists"),
            P("lists"),
            P(),
            P(None, ("lists", "sub")),
            P("sub", None),
            P(None, "sub", "lists"),
        ),
        out_specs=(P("sub", None), P("sub", "lists")),
        check_vma=False,
    )
```

```python
import functools

import jax
import jax.numpy as jnp
from jax import lax
from jax.experimental import pallas as pl
from jax.experimental.pallas import tpu as pltpu
from jax.sharding import PartitionSpec as P

K = 256
DS = 8
LISTS_DEV = 64
ITERS = 2


def shards(vectors, list_ids, counts, coarse, codebook_init, codes):
    features, rows = vectors.shape
    owners = lax.axis_size("lists")
    owner = lax.axis_index("lists")
    block = rows // owners
    subspaces = features // DS
    mine = lax.all_to_all(coarse, "sub", split_axis=0, concat_axis=1, tiled=True)
    list_iota = jnp.arange(LISTS_DEV, dtype=jnp.int32)
    arrived = lax.all_to_all(vectors, "lists", split_axis=1, concat_axis=1, tiled=True)
    labels = lax.all_to_all(
        list_ids.reshape(1, rows), "lists", split_axis=1, concat_axis=1, tiled=True
    ).reshape(rows)
    selector = (labels[None, :] == list_iota[:, None]).astype(jnp.bfloat16)
    centre = jnp.dot(mine, selector, preferred_element_type=jnp.float32)
    residual = (arrived.astype(jnp.float32) - centre).astype(jnp.bfloat16)
    block_counts = lax.dynamic_index_in_dim(counts, owner, 1, keepdims=False)
    valid = (jnp.arange(block, dtype=jnp.int32)[None, :] < block_counts[:, None]).reshape(rows)
    code_iota = jnp.arange(K, dtype=jnp.int32)
    split_res = residual.reshape(subspaces, DS, rows)
    group_size = 4
    groups = subspaces // group_size
    grouped_res = split_res.reshape(groups, group_size, DS, rows)
    grouped_codes = jnp.swapaxes(codes, 0, 1).reshape(groups, group_size, ITERS, rows)

    def group_sums(packed):
        sub_res, sub_codes = packed
        one_hot = (sub_codes[:, :, None, :] == code_iota[None, None, :, None]) & valid[
            None, None, None, :
        ]
        one_hot = one_hot.astype(jnp.bfloat16)
        sums = jnp.einsum("gdr,gtkr->tgdk", sub_res, one_hot, preferred_element_type=jnp.float32)
        tally = jnp.swapaxes(jnp.sum(one_hot, axis=3, dtype=jnp.float32), 0, 1)
        return (sums, tally)

    part_sums, part_counts = lax.map(group_sums, (grouped_res, grouped_codes))
    part_sums = jnp.swapaxes(part_sums, 0, 1).reshape(ITERS, features, K)
    part_counts = jnp.swapaxes(part_counts, 0, 1).reshape(ITERS, subspaces, K)
    weight = 0.25 * jnp.sum(counts).astype(jnp.float32) / K
    total_sums, total_counts = lax.psum((part_sums, part_counts), "lists")
    codebook = codebook_init
    for iteration in range(ITERS):
        spread = jnp.repeat(total_counts[iteration], DS, axis=0)
        codebook = (total_sums[iteration] + weight * codebook) / (spread + weight)
    high = codebook.astype(jnp.bfloat16)
    low = (codebook - high.astype(jnp.float32)).astype(jnp.bfloat16)
    books = jnp.concatenate(
        [high.reshape(subspaces, DS, K), low.reshape(subspaces, DS, K)], axis=1
    ).reshape(groups, group_size, 2 * DS, K)

    def group_pick(packed):
        book, sub_codes = packed
        one_hot = (sub_codes[:, None, :] == code_iota[None, :, None]).astype(jnp.bfloat16)
        both = jnp.einsum("gdk,gkr->gdr", book, one_hot, preferred_element_type=jnp.float32)
        return both[:, :DS] + both[:, DS:]

    picked = lax.map(group_pick, (books, grouped_codes[:, :, ITERS - 1]))
    picked = picked.reshape(subspaces, DS, rows)
    leftover = jnp.where(valid[None, None, :], split_res.astype(jnp.float32) - picked, 0.0)
    leftover = leftover.astype(jnp.bfloat16).reshape(features, rows)
    return (codebook, leftover)


def remote(src, dst, send_sem, recv_sem, device):
    return pltpu.make_async_remote_copy(
        src_ref=src,
        dst_ref=dst,
        send_sem=send_sem,
        recv_sem=recv_sem,
        device_id=device,
        device_id_type=pl.DeviceIdType.MESH,
    )


def kernel(
    owners, subs, vectors, list_ids, counts, own_coarse, init_hbm, codes,
    book_out, left_out,
    vec, coarse, init, hot, arrived, centres, res, parts_out, parts_in, total, books,
    vec_send, vec_recv, cen_send, cen_recv, part_send, part_recv, book_send, book_recv,
    init_sem,
):
    me = lax.axis_index("lists")
    my_sub = lax.axis_index("sub")
    features, rows = res.shape
    cap = vec.shape[1] // 2
    spaces = features // DS
    pieces = features // DS // owners
    height = pieces * DS

    def after(d):
        return lax.rem(me + d, owners)

    def before(d):
        return lax.rem(me + owners - d, owners)

    def sub_after(d):
        return lax.rem(my_sub + d, subs)

    barrier = pltpu.get_barrier_semaphore()

    @pl.loop(1, owners)
    def _(d):
        pl.semaphore_signal(
            barrier, inc=1, device_id={"lists": after(d)}, device_id_type=pl.DeviceIdType.MESH
        )

    for d in range(1, subs):
        pl.semaphore_signal(
            barrier, inc=1, device_id={"sub": sub_after(d)}, device_id_type=pl.DeviceIdType.MESH
        )
    init_copy = pltpu.make_async_copy(init_hbm, init, init_sem)
    init_copy.start()
    turned = own_coarse[...].astype(jnp.float32).T
    for q in range(subs):
        coarse[q] = turned[:, q * features : (q + 1) * features].astype(jnp.bfloat16)
    half = vec.shape[2]
    tail = jnp.broadcast_to(list_ids[...].astype(jnp.float32), (2 * half - features, rows))
    slots = jnp.concatenate([vectors[...].astype(jnp.float32), tail], axis=0).T
    for s in range(owners):
        slot = slots[s * cap : (s + 1) * cap]
        vec[s] = jnp.concatenate([slot[:, :half], slot[:, half:]], axis=0).astype(jnp.bfloat16)
    pl.semaphore_wait(barrier, owners - 1 + subs - 1)

    def cen_copy(q, slot):
        return remote(
            coarse.at[q], centres.at[slot], cen_send.at[q], cen_recv.at[slot], {"sub": q}
        )

    def vec_copy(p, slot):
        return remote(
            vec.at[p], arrived.at[slot], vec_send.at[p], vec_recv.at[slot], {"lists": p}
        )

    def part_copy(p, slot):
        return remote(
            parts_out.at[p], parts_in.at[slot], part_send.at[p], part_recv.at[slot], {"lists": p}
        )

    def book_copy(p, slot):
        return remote(
            books.at[me], books.at[slot], book_send.at[p], book_recv.at[slot], {"lists": p}
        )

    for d in range(1, subs):
        cen_copy(sub_after(d), my_sub).start()

    @pl.loop(1, owners)
    def _(d):
        vec_copy(after(d), me).start()

    arrived[me] = vec[me]
    centres[my_sub] = coarse[my_sub]
    iota = lax.broadcasted_iota(jnp.int32, (16, rows), 0).astype(jnp.float32)

    @pl.loop(0, spaces)
    def _(m):
        for t in range(ITERS):
            code = codes[t, pl.ds(m, 1), :].astype(jnp.float32)
            code = jnp.broadcast_to(code, (16, rows)).astype(jnp.bfloat16)
            for k in range(0, K, 16):
                same = code == (iota + k).astype(jnp.bfloat16)
                hot[t * spaces + m, k : k + 16, :] = jnp.where(
                    same, jnp.ones_like(code), jnp.zeros_like(code)
                )

    tallies = counts[...]
    line = lax.broadcasted_iota(jnp.int32, tallies.shape, 1)
    senders = jnp.sum(
        jnp.where(line == me, tallies, 0).astype(jnp.float32), axis=1, keepdims=True
    )
    first = lax.broadcasted_iota(jnp.int32, (owners, rows), 0) * cap
    place = (lax.broadcasted_iota(jnp.int32, (owners, rows), 1) - first).astype(jnp.float32)
    inside = jnp.where(place >= 0.0, 1.0, 0.0) * jnp.where(place < senders, 1.0, 0.0)
    used = jnp.max(inside, axis=0, keepdims=True)
    every = jnp.sum(tallies.astype(jnp.float32), axis=1, keepdims=True)
    scale = 0.25 * jnp.sum(every, axis=0, keepdims=True) / K

    for d in range(1, subs):
        q = sub_after(d)
        cen_copy(q, q).wait_recv()

    @pl.loop(1, owners)
    def _(d):
        p = before(d)
        vec_copy(p, p).wait_recv()

    slab = arrived[...].astype(jnp.float32)
    full = jnp.concatenate(
        [slab[:, :cap].reshape(rows, half), slab[:, cap:].reshape(rows, half)], axis=1
    )
    labels = full[:, features:]
    lanes = lax.broadcasted_iota(jnp.int32, labels.shape, 1).astype(jnp.float32)
    selector = (labels == lanes).astype(jnp.float32).astype(jnp.bfloat16)
    lists = centres[...].reshape(subs * centres.shape[1], features)
    lists = jnp.concatenate(
        [lists, jnp.zeros((labels.shape[1] - lists.shape[0], features), lists.dtype)], axis=0
    )
    centre = jnp.dot(selector, lists, preferred_element_type=jnp.float32)
    residual = (full[:, :features] - centre).astype(jnp.bfloat16).astype(jnp.float32)
    res[...] = jnp.where(used > 0.0, residual.T, 0.0)

    def one_hot(t, m):
        return hot[t * spaces + m]

    def rows_of(m):
        return pl.ds(pl.multiple_of(m * DS, DS), DS)

    def part(p, t):
        sums = []
        tally = jnp.zeros((DS, K), jnp.float32)
        line = lax.broadcasted_iota(jnp.int32, (DS, K), 0)
        for j in range(pieces):
            m = p * pieces + j
            left = jnp.concatenate(
                [res[rows_of(m), :], jnp.broadcast_to(used, (DS, rows))], axis=0
            ).astype(jnp.bfloat16)
            both = lax.dot_general(
                left, one_hot(t, m), (((1,), (1,)), ((), ())),
                preferred_element_type=jnp.float32,
            )
            sums.append(both[:DS])
            number = both[DS:]
            coarse_part = jnp.floor(number * (1.0 / 128.0)) * 128.0
            tally = jnp.where(line == j, coarse_part, tally)
            tally = jnp.where(line == pieces + j, number - coarse_part, tally)
        return jnp.concatenate(sums + [tally], axis=0)

    @pl.loop(1, owners)
    def _(d):
        p = after(d)
        for t in range(ITERS):
            parts_out[p, t] = part(p, t).astype(jnp.bfloat16)
        part_copy(p, me).start()

    for t in range(ITERS):
        total[t] = part(me, t)

    @pl.loop(1, owners)
    def _(d):
        p = before(d)
        part_copy(p, p).wait_recv()
        for t in range(ITERS):
            total[t] += parts_in[p, t].astype(jnp.float32)

    init_copy.wait()
    mine = []
    for j in range(pieces):
        book = init[rows_of(me * pieces + j), :]
        for t in range(ITERS):
            number = (
                total[t, height + j : height + j + 1]
                + total[t, height + pieces + j : height + pieces + j + 1]
            )
            book = (total[t, j * DS : (j + 1) * DS] + scale * book) / (number + scale)
        mine.append(book)
    mine = jnp.concatenate(mine, axis=0)
    books[me] = jnp.concatenate([mine[:, : K // 2], mine[:, K // 2 :]], axis=0).astype(
        jnp.bfloat16
    )

    @pl.loop(1, owners)
    def _(d):
        book_copy(after(d), me).start()

    def finish(p):
        pair = books[p].astype(jnp.float32)
        book = jnp.concatenate([pair[:height], pair[height:]], axis=1)
        for j in range(pieces):
            m = p * pieces + j
            own = book[j * DS : (j + 1) * DS]
            book_out[rows_of(m), :] = own
            picked = jnp.dot(
                own.astype(jnp.bfloat16), one_hot(ITERS - 1, m),
                preferred_element_type=jnp.float32,
            )
            res[rows_of(m), :] = jnp.where(used > 0.0, res[rows_of(m), :] - picked, 0.0)

    finish(me)

    @pl.loop(1, owners)
    def _(d):
        p = before(d)
        book_copy(p, p).wait_recv()
        finish(p)

    left_out[...] = res[...].astype(jnp.bfloat16)

    for d in range(1, subs):
        cen_copy(sub_after(d), my_sub).wait_send()

    @pl.loop(1, owners)
    def _(d):
        p = after(d)
        vec_copy(p, me).wait_send()
        part_copy(p, me).wait_send()
        book_copy(p, me).wait_send()


def fused(vectors, list_ids, counts, coarse, codebook_init, codes):
    features, rows = vectors.shape
    owners = lax.axis_size("lists")
    subs = lax.axis_size("sub")
    cap = rows // owners
    height = features // owners
    half = (features + 128) // 2
    vec = (owners, 2 * cap, half)
    slabs = (subs, coarse.shape[1], features)
    vmem = pl.BlockSpec(memory_space=pltpu.VMEM)
    dma = pltpu.SemaphoreType.DMA
    part = (owners, ITERS, height + DS, K)
    return pl.pallas_call(
        functools.partial(kernel, owners, subs),
        out_shape=(
            jax.ShapeDtypeStruct((features, K), jnp.float32),
            jax.ShapeDtypeStruct((features, rows), jnp.bfloat16),
        ),
        in_specs=[vmem] * 4 + [pl.BlockSpec(memory_space=pl.ANY), vmem],
        out_specs=(vmem, vmem),
        scratch_shapes=[
            pltpu.VMEM(vec, jnp.bfloat16),
            pltpu.VMEM(slabs, jnp.bfloat16),
            pltpu.VMEM((features, K), jnp.float32),
            pltpu.VMEM((ITERS * features // DS, K, rows), jnp.bfloat16),
            pltpu.VMEM(vec, jnp.bfloat16),
            pltpu.VMEM(slabs, jnp.bfloat16),
            pltpu.VMEM((features, rows), jnp.float32),
            pltpu.VMEM(part, jnp.bfloat16),
            pltpu.VMEM(part, jnp.bfloat16),
            pltpu.VMEM(part[1:], jnp.float32),
            pltpu.VMEM((owners, 2 * height, K // 2), jnp.bfloat16),
            dma((owners,)), dma((owners,)), dma((subs,)), dma((subs,)),
            dma((owners,)), dma((owners,)), dma((owners,)), dma((owners,)),
            dma,
        ],
        compiler_params=pltpu.CompilerParams(
            collective_id=0, has_side_effects=True, vmem_limit_bytes=52 * 1024 * 1024
        ),
    )(vectors, list_ids.reshape(1, rows), counts, coarse, codebook_init, codes)


def fits(owners, subs, vectors, coarse):
    features = vectors.shape[0] // subs
    rows = vectors.shape[1] // owners
    spaces = features // DS
    per = coarse.shape[1] // (owners * subs)
    return (
        features % 256 == 128
        and spaces % owners == 0
        and 2 * (spaces // owners) <= DS
        and (features // owners + DS) % 16 == 0
        and (rows // owners) % DS == 0
        and per % 16 == 0
        and per * subs <= 128
    )


def dispatch(owners, subs, *args):
    whole_features = args[0].shape[0] * subs
    sizes = (
        jax.ShapeDtypeStruct((whole_features, args[0].shape[1] * owners), jnp.bfloat16),
        jax.ShapeDtypeStruct((whole_features, args[3].shape[1] * owners * subs), jnp.bfloat16),
    )
    return (fused if fits(owners, subs, *sizes) else shards)(*args)


def solution(mesh):
    return jax.shard_map(
        functools.partial(dispatch, mesh.shape["lists"], mesh.shape["sub"]),
        mesh=mesh,
        in_specs=(
            P("sub", "lists"),
            P("lists"),
            P(),
            P(None, ("lists", "sub")),
            P("sub", None),
            P(None, "sub", "lists"),
        ),
        out_specs=(P("sub", None), P("sub", "lists")),
        check_vma=False,
    )
```

```python
import functools

import jax
import jax.numpy as jnp
from jax import lax
from jax.experimental import pallas as pl
from jax.experimental.pallas import tpu as pltpu
from jax.sharding import PartitionSpec as P

K = 256
DS = 8
LISTS_DEV = 64
ITERS = 2


def shards(vectors, list_ids, counts, coarse, codebook_init, codes):
    features, rows = vectors.shape
    owners = lax.axis_size("lists")
    owner = lax.axis_index("lists")
    block = rows // owners
    subspaces = features // DS
    mine = lax.all_to_all(coarse, "sub", split_axis=0, concat_axis=1, tiled=True)
    list_iota = jnp.arange(LISTS_DEV, dtype=jnp.int32)
    arrived = lax.all_to_all(vectors, "lists", split_axis=1, concat_axis=1, tiled=True)
    labels = lax.all_to_all(
        list_ids.reshape(1, rows), "lists", split_axis=1, concat_axis=1, tiled=True
    ).reshape(rows)
    selector = (labels[None, :] == list_iota[:, None]).astype(jnp.bfloat16)
    centre = jnp.dot(mine, selector, preferred_element_type=jnp.float32)
    residual = (arrived.astype(jnp.float32) - centre).astype(jnp.bfloat16)
    block_counts = lax.dynamic_index_in_dim(counts, owner, 1, keepdims=False)
    valid = (jnp.arange(block, dtype=jnp.int32)[None, :] < block_counts[:, None]).reshape(rows)
    code_iota = jnp.arange(K, dtype=jnp.int32)
    split_res = residual.reshape(subspaces, DS, rows)
    group_size = 4
    groups = subspaces // group_size
    grouped_res = split_res.reshape(groups, group_size, DS, rows)
    grouped_codes = jnp.swapaxes(codes, 0, 1).reshape(groups, group_size, ITERS, rows)

    def group_sums(packed):
        sub_res, sub_codes = packed
        one_hot = (sub_codes[:, :, None, :] == code_iota[None, None, :, None]) & valid[
            None, None, None, :
        ]
        one_hot = one_hot.astype(jnp.bfloat16)
        sums = jnp.einsum("gdr,gtkr->tgdk", sub_res, one_hot, preferred_element_type=jnp.float32)
        tally = jnp.swapaxes(jnp.sum(one_hot, axis=3, dtype=jnp.float32), 0, 1)
        return (sums, tally)

    part_sums, part_counts = lax.map(group_sums, (grouped_res, grouped_codes))
    part_sums = jnp.swapaxes(part_sums, 0, 1).reshape(ITERS, features, K)
    part_counts = jnp.swapaxes(part_counts, 0, 1).reshape(ITERS, subspaces, K)
    weight = 0.25 * jnp.sum(counts).astype(jnp.float32) / K
    total_sums, total_counts = lax.psum((part_sums, part_counts), "lists")
    codebook = codebook_init
    for iteration in range(ITERS):
        spread = jnp.repeat(total_counts[iteration], DS, axis=0)
        codebook = (total_sums[iteration] + weight * codebook) / (spread + weight)
    high = codebook.astype(jnp.bfloat16)
    low = (codebook - high.astype(jnp.float32)).astype(jnp.bfloat16)
    books = jnp.concatenate(
        [high.reshape(subspaces, DS, K), low.reshape(subspaces, DS, K)], axis=1
    ).reshape(groups, group_size, 2 * DS, K)

    def group_pick(packed):
        book, sub_codes = packed
        one_hot = (sub_codes[:, None, :] == code_iota[None, :, None]).astype(jnp.bfloat16)
        both = jnp.einsum("gdk,gkr->gdr", book, one_hot, preferred_element_type=jnp.float32)
        return both[:, :DS] + both[:, DS:]

    picked = lax.map(group_pick, (books, grouped_codes[:, :, ITERS - 1]))
    picked = picked.reshape(subspaces, DS, rows)
    leftover = jnp.where(valid[None, None, :], split_res.astype(jnp.float32) - picked, 0.0)
    leftover = leftover.astype(jnp.bfloat16).reshape(features, rows)
    return (codebook, leftover)


def remote(src, dst, send_sem, recv_sem, device):
    return pltpu.make_async_remote_copy(
        src_ref=src,
        dst_ref=dst,
        send_sem=send_sem,
        recv_sem=recv_sem,
        device_id=device,
        device_id_type=pl.DeviceIdType.MESH,
    )


def kernel(
    owners, subs, vectors_hbm, list_ids, counts, coarse_hbm, init_hbm, codes_hbm,
    book_out, left_out,
    vectors, own_coarse, codes,
    vec, coarse, init, hot, arrived, centres, res, pair_out, pair_in, kept, parts_out, parts_in,
    total, books,
    vec_send, vec_recv, cen_send, cen_recv, part_send, part_recv, book_send, book_recv,
    pair_send, pair_recv, load_sem,
):
    me = lax.axis_index("lists")
    my_sub = lax.axis_index("sub")
    features, rows = res.shape
    cap = rows // owners
    chips = owners // 2
    core = lax.rem(me, 2)
    chip = me // 2
    partner = chip * 2 + 1 - core
    spaces = features // DS
    pieces = features // DS // owners
    height = pieces * DS

    def after(d):
        return lax.rem(me + d, owners)

    def before(d):
        return lax.rem(me + owners - d, owners)

    def sub_after(d):
        return lax.rem(my_sub + d, subs)

    loads = [
        pltpu.make_async_copy(src, dst, load_sem.at[i])
        for i, (src, dst) in enumerate(
            ((vectors_hbm, vectors), (coarse_hbm, own_coarse), (codes_hbm, codes), (init_hbm, init))
        )
    ]
    for load in loads:
        load.start()

    barrier = pltpu.get_barrier_semaphore()

    @pl.loop(1, owners)
    def _(d):
        pl.semaphore_signal(
            barrier, inc=1, device_id={"lists": after(d)}, device_id_type=pl.DeviceIdType.MESH
        )

    for d in range(1, subs):
        pl.semaphore_signal(
            barrier, inc=1, device_id={"sub": sub_after(d)}, device_id_type=pl.DeviceIdType.MESH
        )
    loads[0].wait()
    loads[1].wait()
    turned = own_coarse[...].astype(jnp.float32).T
    for q in range(subs):
        coarse[q] = turned[:, q * features : (q + 1) * features].astype(jnp.bfloat16)
    tail = jnp.broadcast_to(list_ids[...].astype(jnp.float32), (128, rows))
    slots = jnp.concatenate([vectors[...].astype(jnp.float32), tail], axis=0).T
    group = lax.broadcasted_iota(jnp.int32, (DS, 128), 1) // 32
    for s in range(owners):
        slot = slots[s * cap : (s + 1) * cap]
        label = jnp.zeros((DS, 128), jnp.float32)
        for i in range(cap // DS):
            label = jnp.where(group == i, slot[i * DS : (i + 1) * DS, features:], label)
        pack = [slot[:, c : c + 128] for c in range(0, features, 128)] + [label]
        vec[s] = jnp.concatenate(pack, axis=0).astype(jnp.bfloat16)
    pl.semaphore_wait(barrier, owners - 1 + subs - 1)

    def cen_copy(q, slot):
        return remote(
            coarse.at[q], centres.at[slot], cen_send.at[q], cen_recv.at[slot], {"sub": q}
        )

    def vec_copy(p, slot):
        return remote(
            vec.at[p], arrived.at[slot], vec_send.at[p], vec_recv.at[slot], {"lists": p}
        )

    def pair_copy(c):
        return remote(
            pair_out.at[c], pair_in.at[c], pair_send.at[c], pair_recv.at[c], {"lists": partner}
        )

    def part_copy(c, slot):
        return remote(
            parts_out.at[c], parts_in.at[slot], part_send.at[c], part_recv.at[slot],
            {"lists": c * 2 + core},
        )

    def chip_after(d):
        return lax.rem(chip + d, chips)

    def book_copy(p, slot):
        return remote(
            books.at[me], books.at[slot], book_send.at[p], book_recv.at[slot], {"lists": p}
        )

    for d in range(1, subs):
        cen_copy(sub_after(d), my_sub).start()

    @pl.loop(1, owners)
    def _(d):
        vec_copy(after(d), me).start()

    arrived[me] = vec[me]
    centres[my_sub] = coarse[my_sub]
    loads[2].wait()
    iota = lax.broadcasted_iota(jnp.int32, (16, rows), 0).astype(jnp.float32)

    @pl.loop(0, spaces)
    def _(m):
        for t in range(ITERS):
            code = codes[t, pl.ds(m, 1), :].astype(jnp.float32)
            code = jnp.broadcast_to(code, (16, rows)).astype(jnp.bfloat16)
            for k in range(0, K, 16):
                same = code == (iota + k).astype(jnp.bfloat16)
                hot[t * spaces + m, k : k + 16, :] = jnp.where(
                    same, jnp.ones_like(code), jnp.zeros_like(code)
                )

    tallies = counts[...]
    line = lax.broadcasted_iota(jnp.int32, tallies.shape, 1)
    senders = jnp.sum(
        jnp.where(line == me, tallies, 0).astype(jnp.float32), axis=1, keepdims=True
    )
    first = lax.broadcasted_iota(jnp.int32, (owners, rows), 0) * cap
    place = (lax.broadcasted_iota(jnp.int32, (owners, rows), 1) - first).astype(jnp.float32)
    inside = jnp.where(place >= 0.0, 1.0, 0.0) * jnp.where(place < senders, 1.0, 0.0)
    used = jnp.max(inside, axis=0, keepdims=True)
    every = jnp.sum(tallies.astype(jnp.float32), axis=1, keepdims=True)
    scale = 0.25 * jnp.sum(every, axis=0, keepdims=True) / K

    for d in range(1, subs):
        q = sub_after(d)
        cen_copy(q, q).wait_recv()

    @pl.loop(1, owners)
    def _(d):
        p = before(d)
        vec_copy(p, p).wait_recv()

    slab = arrived[...].astype(jnp.float32)
    full = jnp.concatenate(
        [
            slab[:, i * cap : (i + 1) * cap].reshape(rows, 128)
            for i in range(features // 128)
        ],
        axis=1,
    )
    packed = slab[:, features // 128 * cap :].reshape(owners * DS, 128)
    labels = jnp.concatenate(
        [
            jnp.broadcast_to(packed[:, i * 32 : i * 32 + 1], packed.shape).reshape(owners, DS, 128)
            for i in range(cap // DS)
        ],
        axis=1,
    ).reshape(rows, 128)
    lanes = lax.broadcasted_iota(jnp.int32, labels.shape, 1).astype(jnp.float32)
    selector = (labels == lanes).astype(jnp.float32).astype(jnp.bfloat16)
    lists = centres[...].reshape(subs * centres.shape[1], features)
    lists = jnp.concatenate(
        [lists, jnp.zeros((labels.shape[1] - lists.shape[0], features), lists.dtype)], axis=0
    )
    centre = jnp.dot(selector, lists, preferred_element_type=jnp.float32)
    residual = (full - centre).astype(jnp.bfloat16).astype(jnp.float32)
    res[...] = jnp.where(used > 0.0, residual.T, 0.0)

    def one_hot(t, m):
        return hot[t * spaces + m]

    def rows_of(m):
        return pl.ds(pl.multiple_of(m * DS, DS), DS)

    def part(p, t):
        sums = []
        tally = jnp.zeros((DS, K), jnp.float32)
        line = lax.broadcasted_iota(jnp.int32, (DS, K), 0)
        for j in range(pieces):
            m = p * pieces + j
            left = jnp.concatenate(
                [res[rows_of(m), :], jnp.broadcast_to(used, (DS, rows))], axis=0
            ).astype(jnp.bfloat16)
            both = lax.dot_general(
                left, one_hot(t, m), (((1,), (1,)), ((), ())),
                preferred_element_type=jnp.float32,
            )
            sums.append(both[:DS])
            number = both[DS:]
            coarse_part = jnp.floor(number * (1.0 / 128.0)) * 128.0
            tally = jnp.where(line == j, coarse_part, tally)
            tally = jnp.where(line == pieces + j, number - coarse_part, tally)
        return jnp.concatenate(sums + [tally], axis=0)

    def compute(d):
        c = chip_after(d)
        for t in range(ITERS):
            pair_out[c, t] = part(c * 2 + 1 - core, t).astype(jnp.bfloat16)
        pair_copy(c).start()
        for t in range(ITERS):
            kept[c, t] = part(c * 2 + core, t)

    compute(1)

    @pl.loop(2, chips + 1)
    def _(d):
        compute(d)
        c = chip_after(d - 1)
        pair_copy(c).wait_recv()
        for t in range(ITERS):
            both = kept[c, t] + pair_in[c, t].astype(jnp.float32)
            parts_out[c, t] = both.astype(jnp.bfloat16)
        part_copy(c, chip).start()

    pair_copy(chip).wait_recv()
    for t in range(ITERS):
        total[t] = kept[chip, t] + pair_in[chip, t].astype(jnp.float32)

    @pl.loop(1, chips)
    def _(d):
        c = lax.rem(chip + chips - d, chips)
        part_copy(c, c).wait_recv()
        for t in range(ITERS):
            total[t] += parts_in[c, t].astype(jnp.float32)

    loads[3].wait()
    mine = []
    for j in range(pieces):
        book = init[rows_of(me * pieces + j), :]
        for t in range(ITERS):
            number = (
                total[t, height + j : height + j + 1]
                + total[t, height + pieces + j : height + pieces + j + 1]
            )
            book = (total[t, j * DS : (j + 1) * DS] + scale * book) / (number + scale)
        mine.append(book)
    mine = jnp.concatenate(mine, axis=0)
    books[me] = jnp.concatenate([mine[:, : K // 2], mine[:, K // 2 :]], axis=0).astype(
        jnp.bfloat16
    )

    @pl.loop(1, owners)
    def _(d):
        book_copy(after(d), me).start()

    def finish(p):
        pair = books[p].astype(jnp.float32)
        book = jnp.concatenate([pair[:height], pair[height:]], axis=1)
        for j in range(pieces):
            m = p * pieces + j
            own = book[j * DS : (j + 1) * DS]
            book_out[rows_of(m), :] = own
            picked = jnp.dot(
                own.astype(jnp.bfloat16), one_hot(ITERS - 1, m),
                preferred_element_type=jnp.float32,
            )
            res[rows_of(m), :] = jnp.where(used > 0.0, res[rows_of(m), :] - picked, 0.0)

    finish(me)

    @pl.loop(1, owners)
    def _(d):
        p = before(d)
        book_copy(p, p).wait_recv()
        finish(p)

    left_out[...] = res[...].astype(jnp.bfloat16)

    for d in range(1, subs):
        cen_copy(sub_after(d), my_sub).wait_send()

    @pl.loop(1, owners)
    def _(d):
        p = after(d)
        vec_copy(p, me).wait_send()
        book_copy(p, me).wait_send()

    @pl.loop(1, chips)
    def _(d):
        part_copy(chip_after(d), chip).wait_send()

    @pl.loop(0, chips)
    def _(c):
        pair_copy(c).wait_send()


def fused(vectors, list_ids, counts, coarse, codebook_init, codes):
    features, rows = vectors.shape
    owners = lax.axis_size("lists")
    subs = lax.axis_size("sub")
    cap = rows // owners
    height = features // owners
    vec = (owners, features // 128 * cap + DS, 128)
    slabs = (subs, coarse.shape[1], features)
    vmem = pl.BlockSpec(memory_space=pltpu.VMEM)
    hbm = pl.BlockSpec(memory_space=pl.ANY)
    dma = pltpu.SemaphoreType.DMA
    part = (owners // 2, ITERS, height + DS, K)
    return pl.pallas_call(
        functools.partial(kernel, owners, subs),
        out_shape=(
            jax.ShapeDtypeStruct((features, K), jnp.float32),
            jax.ShapeDtypeStruct((features, rows), jnp.bfloat16),
        ),
        in_specs=[hbm, vmem, vmem, hbm, hbm, hbm],
        out_specs=(vmem, vmem),
        scratch_shapes=[
            pltpu.VMEM(vectors.shape, jnp.bfloat16),
            pltpu.VMEM(coarse.shape, jnp.bfloat16),
            pltpu.VMEM(codes.shape, jnp.int32),
            pltpu.VMEM(vec, jnp.bfloat16),
            pltpu.VMEM(slabs, jnp.bfloat16),
            pltpu.VMEM((features, K), jnp.float32),
            pltpu.VMEM((ITERS * features // DS, K, rows), jnp.bfloat16),
            pltpu.VMEM(vec, jnp.bfloat16),
            pltpu.VMEM(slabs, jnp.bfloat16),
            pltpu.VMEM((features, rows), jnp.float32),
            pltpu.VMEM(part, jnp.bfloat16),
            pltpu.VMEM(part, jnp.bfloat16),
            pltpu.VMEM(part, jnp.float32),
            pltpu.VMEM(part, jnp.bfloat16),
            pltpu.VMEM(part, jnp.bfloat16),
            pltpu.VMEM(part[1:], jnp.float32),
            pltpu.VMEM((owners, 2 * height, K // 2), jnp.bfloat16),
            dma((owners,)), dma((owners,)), dma((subs,)), dma((subs,)),
            dma((owners // 2,)), dma((owners // 2,)), dma((owners,)), dma((owners,)),
            dma((owners // 2,)), dma((owners // 2,)), dma((4,)),
        ],
        compiler_params=pltpu.CompilerParams(
            collective_id=0, has_side_effects=True, vmem_limit_bytes=60 * 1024 * 1024
        ),
    )(vectors, list_ids.reshape(1, rows), counts, coarse, codebook_init, codes)


def fits(owners, subs, vectors, coarse):
    features = vectors.shape[0] // subs
    rows = vectors.shape[1] // owners
    spaces = features // DS
    per = coarse.shape[1] // (owners * subs)
    return (
        features % 128 == 0
        and owners % 2 == 0
        and rows // owners <= 32
        and (features // 128 * (rows // owners) + DS) % 16 == 0
        and spaces % owners == 0
        and 2 * (spaces // owners) <= DS
        and (features // owners + DS) % 16 == 0
        and (rows // owners) % DS == 0
        and per % 16 == 0
        and per * subs <= 128
    )


def dispatch(owners, subs, *args):
    whole_features = args[0].shape[0] * subs
    sizes = (
        jax.ShapeDtypeStruct((whole_features, args[0].shape[1] * owners), jnp.bfloat16),
        jax.ShapeDtypeStruct((whole_features, args[3].shape[1] * owners * subs), jnp.bfloat16),
    )
    return (fused if fits(owners, subs, *sizes) else shards)(*args)


def solution(mesh):
    return jax.shard_map(
        functools.partial(dispatch, mesh.shape["lists"], mesh.shape["sub"]),
        mesh=mesh,
        in_specs=(
            P("sub", "lists"),
            P("lists"),
            P(),
            P(None, ("lists", "sub")),
            P("sub", None),
            P(None, "sub", "lists"),
        ),
        out_specs=(P("sub", None), P("sub", "lists")),
        check_vma=False,
    )
```

```python
import functools

import jax
import jax.numpy as jnp
from jax import lax
from jax.experimental import pallas as pl
from jax.experimental.pallas import tpu as pltpu
from jax.sharding import PartitionSpec as P

K = 256
DS = 8
LISTS_DEV = 64
ITERS = 2


def shards(vectors, list_ids, counts, coarse, codebook_init, codes):
    features, rows = vectors.shape
    owners = lax.axis_size("lists")
    owner = lax.axis_index("lists")
    block = rows // owners
    subspaces = features // DS
    mine = lax.all_to_all(coarse, "sub", split_axis=0, concat_axis=1, tiled=True)
    list_iota = jnp.arange(LISTS_DEV, dtype=jnp.int32)
    arrived = lax.all_to_all(vectors, "lists", split_axis=1, concat_axis=1, tiled=True)
    labels = lax.all_to_all(
        list_ids.reshape(1, rows), "lists", split_axis=1, concat_axis=1, tiled=True
    ).reshape(rows)
    selector = (labels[None, :] == list_iota[:, None]).astype(jnp.bfloat16)
    centre = jnp.dot(mine, selector, preferred_element_type=jnp.float32)
    residual = (arrived.astype(jnp.float32) - centre).astype(jnp.bfloat16)
    block_counts = lax.dynamic_index_in_dim(counts, owner, 1, keepdims=False)
    valid = (jnp.arange(block, dtype=jnp.int32)[None, :] < block_counts[:, None]).reshape(rows)
    code_iota = jnp.arange(K, dtype=jnp.int32)
    split_res = residual.reshape(subspaces, DS, rows)
    group_size = 4
    groups = subspaces // group_size
    grouped_res = split_res.reshape(groups, group_size, DS, rows)
    grouped_codes = jnp.swapaxes(codes, 0, 1).reshape(groups, group_size, ITERS, rows)

    def group_sums(packed):
        sub_res, sub_codes = packed
        one_hot = (sub_codes[:, :, None, :] == code_iota[None, None, :, None]) & valid[
            None, None, None, :
        ]
        one_hot = one_hot.astype(jnp.bfloat16)
        sums = jnp.einsum("gdr,gtkr->tgdk", sub_res, one_hot, preferred_element_type=jnp.float32)
        tally = jnp.swapaxes(jnp.sum(one_hot, axis=3, dtype=jnp.float32), 0, 1)
        return (sums, tally)

    part_sums, part_counts = lax.map(group_sums, (grouped_res, grouped_codes))
    part_sums = jnp.swapaxes(part_sums, 0, 1).reshape(ITERS, features, K)
    part_counts = jnp.swapaxes(part_counts, 0, 1).reshape(ITERS, subspaces, K)
    weight = 0.25 * jnp.sum(counts).astype(jnp.float32) / K
    total_sums, total_counts = lax.psum((part_sums, part_counts), "lists")
    codebook = codebook_init
    for iteration in range(ITERS):
        spread = jnp.repeat(total_counts[iteration], DS, axis=0)
        codebook = (total_sums[iteration] + weight * codebook) / (spread + weight)
    high = codebook.astype(jnp.bfloat16)
    low = (codebook - high.astype(jnp.float32)).astype(jnp.bfloat16)
    books = jnp.concatenate(
        [high.reshape(subspaces, DS, K), low.reshape(subspaces, DS, K)], axis=1
    ).reshape(groups, group_size, 2 * DS, K)

    def group_pick(packed):
        book, sub_codes = packed
        one_hot = (sub_codes[:, None, :] == code_iota[None, :, None]).astype(jnp.bfloat16)
        both = jnp.einsum("gdk,gkr->gdr", book, one_hot, preferred_element_type=jnp.float32)
        return both[:, :DS] + both[:, DS:]

    picked = lax.map(group_pick, (books, grouped_codes[:, :, ITERS - 1]))
    picked = picked.reshape(subspaces, DS, rows)
    leftover = jnp.where(valid[None, None, :], split_res.astype(jnp.float32) - picked, 0.0)
    leftover = leftover.astype(jnp.bfloat16).reshape(features, rows)
    return (codebook, leftover)


def remote(src, dst, send_sem, recv_sem, device):
    return pltpu.make_async_remote_copy(
        src_ref=src,
        dst_ref=dst,
        send_sem=send_sem,
        recv_sem=recv_sem,
        device_id=device,
        device_id_type=pl.DeviceIdType.MESH,
    )


def kernel(
    owners, subs, vectors_hbm, list_ids, counts, coarse_hbm, init_hbm, codes_hbm,
    book_out, left_out,
    vectors, own_coarse, codes,
    vec, coarse, init, hot, arrived, centres, res, pair_out, pair_in, kept, parts_out, parts_in,
    total, books,
    vec_send, vec_recv, cen_send, cen_recv, part_send, part_recv, book_send, book_recv,
    pair_send, pair_recv, load_sem,
):
    me = lax.axis_index("lists")
    my_sub = lax.axis_index("sub")
    features, rows = res.shape
    cap = rows // owners
    chips = owners // 2
    core = lax.rem(me, 2)
    chip = me // 2
    partner = chip * 2 + 1 - core
    spaces = features // DS
    pieces = features // DS // owners
    height = pieces * DS

    def after(d):
        return lax.rem(me + d, owners)

    def before(d):
        return lax.rem(me + owners - d, owners)

    def sub_after(d):
        return lax.rem(my_sub + d, subs)

    loads = [
        pltpu.make_async_copy(src, dst, load_sem.at[i])
        for i, (src, dst) in enumerate(
            ((vectors_hbm, vectors), (coarse_hbm, own_coarse), (codes_hbm, codes), (init_hbm, init))
        )
    ]
    for load in loads:
        load.start()

    barrier = pltpu.get_barrier_semaphore()

    @pl.loop(1, owners)
    def _(d):
        pl.semaphore_signal(
            barrier, inc=1, device_id={"lists": after(d)}, device_id_type=pl.DeviceIdType.MESH
        )

    for d in range(1, subs):
        pl.semaphore_signal(
            barrier, inc=1, device_id={"sub": sub_after(d)}, device_id_type=pl.DeviceIdType.MESH
        )
    loads[0].wait()
    loads[1].wait()
    for q in range(subs):
        coarse[q] = own_coarse[:, q * features : (q + 1) * features]
    tail = jnp.broadcast_to(list_ids[...].reshape(1, rows).astype(jnp.float32), (128, rows))
    slots = jnp.concatenate([vectors[...].astype(jnp.float32), tail], axis=0).T
    group = lax.broadcasted_iota(jnp.int32, (DS, 128), 1) // 32
    for s in range(owners):
        slot = slots[s * cap : (s + 1) * cap]
        label = jnp.zeros((DS, 128), jnp.float32)
        for i in range(cap // DS):
            label = jnp.where(group == i, slot[i * DS : (i + 1) * DS, features:], label)
        pack = [slot[:, c : c + 128] for c in range(0, features, 128)] + [label]
        vec[s] = jnp.concatenate(pack, axis=0).astype(jnp.bfloat16)
    pl.semaphore_wait(barrier, owners - 1 + subs - 1)

    def cen_copy(q, slot):
        return remote(
            coarse.at[q], centres.at[slot], cen_send.at[q], cen_recv.at[slot], {"sub": q}
        )

    def vec_copy(p, slot):
        return remote(
            vec.at[p], arrived.at[slot], vec_send.at[p], vec_recv.at[slot], {"lists": p}
        )

    def pair_copy(c):
        return remote(
            pair_out.at[c], pair_in.at[c], pair_send.at[c], pair_recv.at[c], {"lists": partner}
        )

    def part_copy(c, slot):
        return remote(
            parts_out.at[c], parts_in.at[slot], part_send.at[c], part_recv.at[slot],
            {"lists": c * 2 + core},
        )

    def chip_after(d):
        return lax.rem(chip + d, chips)

    def book_copy(p, slot):
        return remote(
            books.at[me], books.at[slot], book_send.at[p], book_recv.at[slot], {"lists": p}
        )

    for d in range(1, subs):
        cen_copy(sub_after(d), my_sub).start()

    @pl.loop(1, owners)
    def _(d):
        vec_copy(after(d), me).start()

    arrived[me] = vec[me]
    centres[my_sub] = coarse[my_sub]
    loads[2].wait()
    iota = lax.broadcasted_iota(jnp.int32, (16, rows), 0).astype(jnp.float32)

    @pl.loop(0, spaces)
    def _(m):
        for t in range(ITERS):
            code = codes[t, pl.ds(m, 1), :].astype(jnp.float32)
            code = jnp.broadcast_to(code, (16, rows)).astype(jnp.bfloat16)
            for k in range(0, K, 16):
                same = code == (iota + k).astype(jnp.bfloat16)
                hot[t * spaces + m, k : k + 16, :] = jnp.where(
                    same, jnp.ones_like(code), jnp.zeros_like(code)
                )

    tallies = counts[...]
    line = lax.broadcasted_iota(jnp.int32, tallies.shape, 1)
    senders = jnp.sum(
        jnp.where(line == me, tallies, 0).astype(jnp.float32), axis=1, keepdims=True
    )
    first = lax.broadcasted_iota(jnp.int32, (owners, rows), 0) * cap
    place = (lax.broadcasted_iota(jnp.int32, (owners, rows), 1) - first).astype(jnp.float32)
    inside = jnp.where(place >= 0.0, 1.0, 0.0) * jnp.where(place < senders, 1.0, 0.0)
    used = jnp.max(inside, axis=0, keepdims=True)
    every = jnp.sum(tallies.astype(jnp.float32), axis=1, keepdims=True)
    scale = 0.25 * jnp.sum(every, axis=0, keepdims=True) / K

    for d in range(1, subs):
        q = sub_after(d)
        cen_copy(q, q).wait_recv()

    @pl.loop(1, owners)
    def _(d):
        p = before(d)
        vec_copy(p, p).wait_recv()

    slab = arrived[...].astype(jnp.float32)
    full = jnp.concatenate(
        [
            slab[:, i * cap : (i + 1) * cap].reshape(rows, 128)
            for i in range(features // 128)
        ],
        axis=1,
    )
    packed = slab[:, features // 128 * cap :].reshape(owners * DS, 128)
    labels = jnp.concatenate(
        [
            jnp.broadcast_to(packed[:, i * 32 : i * 32 + 1], packed.shape).reshape(owners, DS, 128)
            for i in range(cap // DS)
        ],
        axis=1,
    ).reshape(rows, 128)
    lanes = lax.broadcasted_iota(jnp.int32, labels.shape, 1).astype(jnp.float32)
    selector = (labels == lanes).astype(jnp.float32).astype(jnp.bfloat16)
    lists = centres[...].reshape(subs * centres.shape[1], features)
    lists = jnp.concatenate(
        [lists, jnp.zeros((labels.shape[1] - lists.shape[0], features), lists.dtype)], axis=0
    )
    centre = jnp.dot(selector, lists, preferred_element_type=jnp.float32)
    residual = (full - centre).astype(jnp.bfloat16).astype(jnp.float32)
    res[...] = jnp.where(used > 0.0, residual.T, 0.0)

    def one_hot(t, m):
        return hot[t * spaces + m]

    def rows_of(m):
        return pl.ds(pl.multiple_of(m * DS, DS), DS)

    def part(p, t):
        sums = []
        tally = jnp.zeros((DS, K), jnp.float32)
        line = lax.broadcasted_iota(jnp.int32, (DS, K), 0)
        for j in range(pieces):
            m = p * pieces + j
            left = jnp.concatenate(
                [res[rows_of(m), :], jnp.broadcast_to(used, (DS, rows))], axis=0
            ).astype(jnp.bfloat16)
            both = lax.dot_general(
                left, one_hot(t, m), (((1,), (1,)), ((), ())),
                preferred_element_type=jnp.float32,
            )
            sums.append(both[:DS])
            number = both[DS:]
            coarse_part = jnp.floor(number * (1.0 / 128.0)) * 128.0
            tally = jnp.where(line == j, coarse_part, tally)
            tally = jnp.where(line == pieces + j, number - coarse_part, tally)
        return jnp.concatenate(sums + [tally], axis=0)

    def compute(d):
        c = chip_after(d)
        for t in range(ITERS):
            pair_out[c, t] = part(c * 2 + 1 - core, t).astype(jnp.bfloat16)
        pair_copy(c).start()
        for t in range(ITERS):
            kept[c, t] = part(c * 2 + core, t)

    compute(1)

    @pl.loop(2, chips + 1)
    def _(d):
        compute(d)
        c = chip_after(d - 1)
        pair_copy(c).wait_recv()
        for t in range(ITERS):
            both = kept[c, t] + pair_in[c, t].astype(jnp.float32)
            parts_out[c, t] = both.astype(jnp.bfloat16)
        part_copy(c, chip).start()

    pair_copy(chip).wait_recv()
    for t in range(ITERS):
        total[t] = kept[chip, t] + pair_in[chip, t].astype(jnp.float32)

    @pl.loop(1, chips)
    def _(d):
        c = lax.rem(chip + chips - d, chips)
        part_copy(c, c).wait_recv()
        for t in range(ITERS):
            total[t] += parts_in[c, t].astype(jnp.float32)

    loads[3].wait()
    mine = []
    for j in range(pieces):
        book = init[rows_of(me * pieces + j), :]
        for t in range(ITERS):
            number = (
                total[t, height + j : height + j + 1]
                + total[t, height + pieces + j : height + pieces + j + 1]
            )
            book = (total[t, j * DS : (j + 1) * DS] + scale * book) / (number + scale)
        mine.append(book)
    mine = jnp.concatenate(mine, axis=0)
    books[me] = jnp.concatenate([mine[:, : K // 2], mine[:, K // 2 :]], axis=0).astype(
        jnp.bfloat16
    )

    @pl.loop(1, owners)
    def _(d):
        book_copy(after(d), me).start()

    def finish(p):
        pair = books[p].astype(jnp.float32)
        book = jnp.concatenate([pair[:height], pair[height:]], axis=1)
        for j in range(pieces):
            m = p * pieces + j
            own = book[j * DS : (j + 1) * DS]
            init[rows_of(m), :] = own
            picked = jnp.dot(
                own.astype(jnp.bfloat16), one_hot(ITERS - 1, m),
                preferred_element_type=jnp.float32,
            )
            res[rows_of(m), :] = jnp.where(used > 0.0, res[rows_of(m), :] - picked, 0.0)

    finish(me)

    @pl.loop(1, owners)
    def _(d):
        p = before(d)
        book_copy(p, p).wait_recv()
        finish(p)

    book_out[...] = init[...].astype(jnp.bfloat16)
    left_out[...] = res[...].astype(jnp.bfloat16)

    for d in range(1, subs):
        cen_copy(sub_after(d), my_sub).wait_send()

    @pl.loop(1, owners)
    def _(d):
        p = after(d)
        vec_copy(p, me).wait_send()
        book_copy(p, me).wait_send()

    @pl.loop(1, chips)
    def _(d):
        part_copy(chip_after(d), chip).wait_send()

    @pl.loop(0, chips)
    def _(c):
        pair_copy(c).wait_send()


def fused(vectors, list_ids, counts, coarse, codebook_init, codes):
    features, rows = vectors.shape
    owners = lax.axis_size("lists")
    subs = lax.axis_size("sub")
    cap = rows // owners
    height = features // owners
    vec = (owners, features // 128 * cap + DS, 128)
    slabs = (subs, coarse.shape[1], features)
    vmem = pl.BlockSpec(memory_space=pltpu.VMEM)
    hbm = pl.BlockSpec(memory_space=pl.ANY)
    dma = pltpu.SemaphoreType.DMA
    part = (owners // 2, ITERS, height + DS, K)
    codebook, leftover = pl.pallas_call(
        functools.partial(kernel, owners, subs),
        out_shape=(
            jax.ShapeDtypeStruct((features, K), jnp.bfloat16),
            jax.ShapeDtypeStruct((features, rows), jnp.bfloat16),
        ),
        in_specs=[hbm, vmem, vmem, hbm, hbm, hbm],
        out_specs=(vmem, vmem),
        scratch_shapes=[
            pltpu.VMEM(vectors.shape, jnp.bfloat16),
            pltpu.VMEM(coarse.shape[::-1], jnp.bfloat16),
            pltpu.VMEM(codes.shape, jnp.int32),
            pltpu.VMEM(vec, jnp.bfloat16),
            pltpu.VMEM(slabs, jnp.bfloat16),
            pltpu.VMEM((features, K), jnp.float32),
            pltpu.VMEM((ITERS * features // DS, K, rows), jnp.bfloat16),
            pltpu.VMEM(vec, jnp.bfloat16),
            pltpu.VMEM(slabs, jnp.bfloat16),
            pltpu.VMEM((features, rows), jnp.float32),
            pltpu.VMEM(part, jnp.bfloat16),
            pltpu.VMEM(part, jnp.bfloat16),
            pltpu.VMEM(part, jnp.float32),
            pltpu.VMEM(part, jnp.bfloat16),
            pltpu.VMEM(part, jnp.bfloat16),
            pltpu.VMEM(part[1:], jnp.float32),
            pltpu.VMEM((owners, 2 * height, K // 2), jnp.bfloat16),
            dma((owners,)), dma((owners,)), dma((subs,)), dma((subs,)),
            dma((owners // 2,)), dma((owners // 2,)), dma((owners,)), dma((owners,)),
            dma((owners // 2,)), dma((owners // 2,)), dma((4,)),
        ],
        compiler_params=pltpu.CompilerParams(
            collective_id=0, has_side_effects=True, vmem_limit_bytes=60 * 1024 * 1024
        ),
    )(vectors, list_ids, counts, coarse.T, codebook_init, codes)
    return (codebook.astype(jnp.float32), leftover)


def fits(owners, subs, vectors, coarse):
    features = vectors.shape[0] // subs
    rows = vectors.shape[1] // owners
    spaces = features // DS
    per = coarse.shape[1] // (owners * subs)
    return (
        features % 128 == 0
        and owners % 2 == 0
        and rows // owners <= 32
        and (features // 128 * (rows // owners) + DS) % 16 == 0
        and spaces % owners == 0
        and 2 * (spaces // owners) <= DS
        and (features // owners + DS) % 16 == 0
        and (rows // owners) % DS == 0
        and per % 16 == 0
        and per * subs <= 128
    )


def dispatch(owners, subs, *args):
    whole_features = args[0].shape[0] * subs
    sizes = (
        jax.ShapeDtypeStruct((whole_features, args[0].shape[1] * owners), jnp.bfloat16),
        jax.ShapeDtypeStruct((whole_features, args[3].shape[1] * owners * subs), jnp.bfloat16),
    )
    return (fused if fits(owners, subs, *sizes) else shards)(*args)


def solution(mesh):
    return jax.shard_map(
        functools.partial(dispatch, mesh.shape["lists"], mesh.shape["sub"]),
        mesh=mesh,
        in_specs=(
            P("sub", "lists"),
            P("lists"),
            P(),
            P(None, ("lists", "sub")),
            P("sub", None),
            P(None, "sub", "lists"),
        ),
        out_specs=(P("sub", None), P("sub", "lists")),
        check_vma=False,
    )
```

```python
import functools

import jax
import jax.numpy as jnp
from jax import lax
from jax.experimental import pallas as pl
from jax.experimental.pallas import tpu as pltpu
from jax.sharding import PartitionSpec as P

K = 256
DS = 8
LISTS_DEV = 64
ITERS = 2


def shards(vectors, list_ids, counts, coarse, codebook_init, codes):
    features, rows = vectors.shape
    owners = lax.axis_size("lists")
    owner = lax.axis_index("lists")
    block = rows // owners
    subspaces = features // DS
    mine = lax.all_to_all(coarse, "sub", split_axis=0, concat_axis=1, tiled=True)
    list_iota = jnp.arange(LISTS_DEV, dtype=jnp.int32)
    arrived = lax.all_to_all(vectors, "lists", split_axis=1, concat_axis=1, tiled=True)
    labels = lax.all_to_all(
        list_ids.reshape(1, rows), "lists", split_axis=1, concat_axis=1, tiled=True
    ).reshape(rows)
    selector = (labels[None, :] == list_iota[:, None]).astype(jnp.bfloat16)
    centre = jnp.dot(mine, selector, preferred_element_type=jnp.float32)
    residual = (arrived.astype(jnp.float32) - centre).astype(jnp.bfloat16)
    block_counts = lax.dynamic_index_in_dim(counts, owner, 1, keepdims=False)
    valid = (jnp.arange(block, dtype=jnp.int32)[None, :] < block_counts[:, None]).reshape(rows)
    code_iota = jnp.arange(K, dtype=jnp.int32)
    split_res = residual.reshape(subspaces, DS, rows)
    group_size = 4
    groups = subspaces // group_size
    grouped_res = split_res.reshape(groups, group_size, DS, rows)
    grouped_codes = jnp.swapaxes(codes, 0, 1).reshape(groups, group_size, ITERS, rows)

    def group_sums(packed):
        sub_res, sub_codes = packed
        one_hot = (sub_codes[:, :, None, :] == code_iota[None, None, :, None]) & valid[
            None, None, None, :
        ]
        one_hot = one_hot.astype(jnp.bfloat16)
        sums = jnp.einsum("gdr,gtkr->tgdk", sub_res, one_hot, preferred_element_type=jnp.float32)
        tally = jnp.swapaxes(jnp.sum(one_hot, axis=3, dtype=jnp.float32), 0, 1)
        return (sums, tally)

    part_sums, part_counts = lax.map(group_sums, (grouped_res, grouped_codes))
    part_sums = jnp.swapaxes(part_sums, 0, 1).reshape(ITERS, features, K)
    part_counts = jnp.swapaxes(part_counts, 0, 1).reshape(ITERS, subspaces, K)
    weight = 0.25 * jnp.sum(counts).astype(jnp.float32) / K
    total_sums, total_counts = lax.psum((part_sums, part_counts), "lists")
    codebook = codebook_init
    for iteration in range(ITERS):
        spread = jnp.repeat(total_counts[iteration], DS, axis=0)
        codebook = (total_sums[iteration] + weight * codebook) / (spread + weight)
    high = codebook.astype(jnp.bfloat16)
    low = (codebook - high.astype(jnp.float32)).astype(jnp.bfloat16)
    books = jnp.concatenate(
        [high.reshape(subspaces, DS, K), low.reshape(subspaces, DS, K)], axis=1
    ).reshape(groups, group_size, 2 * DS, K)

    def group_pick(packed):
        book, sub_codes = packed
        one_hot = (sub_codes[:, None, :] == code_iota[None, :, None]).astype(jnp.bfloat16)
        both = jnp.einsum("gdk,gkr->gdr", book, one_hot, preferred_element_type=jnp.float32)
        return both[:, :DS] + both[:, DS:]

    picked = lax.map(group_pick, (books, grouped_codes[:, :, ITERS - 1]))
    picked = picked.reshape(subspaces, DS, rows)
    leftover = jnp.where(valid[None, None, :], split_res.astype(jnp.float32) - picked, 0.0)
    leftover = leftover.astype(jnp.bfloat16).reshape(features, rows)
    return (codebook, leftover)


def remote(src, dst, send_sem, recv_sem, device):
    return pltpu.make_async_remote_copy(
        src_ref=src,
        dst_ref=dst,
        send_sem=send_sem,
        recv_sem=recv_sem,
        device_id=device,
        device_id_type=pl.DeviceIdType.MESH,
    )


def kernel(
    owners, subs, vectors_hbm, list_ids, counts, coarse_hbm, init_hbm, codes_hbm,
    book_out, left_out,
    vectors, own_coarse, codes,
    vec, coarse, init, hot, arrived, centres, res, pair_out, pair_in, kept, parts_out, parts_in,
    total, books,
    vec_send, vec_recv, cen_send, cen_recv, part_send, part_recv, book_send, book_recv,
    pair_send, pair_recv, load_sem,
):
    me = lax.axis_index("lists")
    my_sub = lax.axis_index("sub")
    features, rows = res.shape
    cap = rows // owners
    chips = owners // 2
    core = lax.rem(me, 2)
    chip = me // 2
    partner = chip * 2 + 1 - core
    spaces = features // DS
    pieces = features // DS // owners
    height = pieces * DS

    def spread(d, size):
        return size // 2 + lax.div(d, 2) * (1 - 2 * lax.rem(d, 2))

    def after(d):
        return lax.rem(me + spread(d, owners), owners)

    def before(d):
        return lax.rem(me + owners - spread(d, owners), owners)

    def sub_after(d):
        return lax.rem(my_sub + d, subs)

    loads = [
        pltpu.make_async_copy(src, dst, load_sem.at[i])
        for i, (src, dst) in enumerate(
            ((vectors_hbm, vectors), (coarse_hbm, own_coarse), (codes_hbm, codes), (init_hbm, init))
        )
    ]
    for load in loads:
        load.start()

    barrier = pltpu.get_barrier_semaphore()

    @pl.loop(1, owners)
    def _(d):
        pl.semaphore_signal(
            barrier, inc=1, device_id={"lists": after(d)}, device_id_type=pl.DeviceIdType.MESH
        )

    for d in range(1, subs):
        pl.semaphore_signal(
            barrier, inc=1, device_id={"sub": sub_after(d)}, device_id_type=pl.DeviceIdType.MESH
        )
    loads[0].wait()
    loads[1].wait()
    for q in range(subs):
        coarse[q] = own_coarse[:, q * features : (q + 1) * features]
    tail = jnp.broadcast_to(list_ids[...].reshape(1, rows).astype(jnp.float32), (128, rows))
    slots = jnp.concatenate([vectors[...].astype(jnp.float32), tail], axis=0).T
    group = lax.broadcasted_iota(jnp.int32, (DS, 128), 1) // 32
    for s in range(owners):
        slot = slots[s * cap : (s + 1) * cap]
        label = jnp.zeros((DS, 128), jnp.float32)
        for i in range(cap // DS):
            label = jnp.where(group == i, slot[i * DS : (i + 1) * DS, features:], label)
        pack = [slot[:, c : c + 128] for c in range(0, features, 128)] + [label]
        vec[s] = jnp.concatenate(pack, axis=0).astype(jnp.bfloat16)
    pl.semaphore_wait(barrier, owners - 1 + subs - 1)

    def cen_copy(q, slot):
        return remote(
            coarse.at[q], centres.at[slot], cen_send.at[q], cen_recv.at[slot], {"sub": q}
        )

    def vec_copy(p, slot):
        return remote(
            vec.at[p], arrived.at[slot], vec_send.at[p], vec_recv.at[slot], {"lists": p}
        )

    def pair_copy(c):
        return remote(
            pair_out.at[c], pair_in.at[c], pair_send.at[c], pair_recv.at[c], {"lists": partner}
        )

    def part_copy(c, slot):
        return remote(
            parts_out.at[c], parts_in.at[slot], part_send.at[c], part_recv.at[slot],
            {"lists": c * 2 + core},
        )

    def chip_after(d):
        return lax.rem(chip + spread(d, chips), chips)

    def book_copy(p, slot):
        return remote(
            books.at[me], books.at[slot], book_send.at[p], book_recv.at[slot], {"lists": p}
        )

    for d in range(1, subs):
        cen_copy(sub_after(d), my_sub).start()

    @pl.loop(1, owners)
    def _(d):
        vec_copy(after(d), me).start()

    arrived[me] = vec[me]
    centres[my_sub] = coarse[my_sub]
    loads[2].wait()
    iota = lax.broadcasted_iota(jnp.int32, (16, rows), 0).astype(jnp.float32)

    @pl.loop(0, spaces)
    def _(m):
        for t in range(ITERS):
            code = codes[t, pl.ds(m, 1), :].astype(jnp.float32)
            code = jnp.broadcast_to(code, (16, rows)).astype(jnp.bfloat16)
            for k in range(0, K, 16):
                same = code == (iota + k).astype(jnp.bfloat16)
                hot[t * spaces + m, k : k + 16, :] = jnp.where(
                    same, jnp.ones_like(code), jnp.zeros_like(code)
                )

    tallies = counts[...]
    line = lax.broadcasted_iota(jnp.int32, tallies.shape, 1)
    senders = jnp.sum(
        jnp.where(line == me, tallies, 0).astype(jnp.float32), axis=1, keepdims=True
    )
    first = lax.broadcasted_iota(jnp.int32, (owners, rows), 0) * cap
    place = (lax.broadcasted_iota(jnp.int32, (owners, rows), 1) - first).astype(jnp.float32)
    inside = jnp.where(place >= 0.0, 1.0, 0.0) * jnp.where(place < senders, 1.0, 0.0)
    used = jnp.max(inside, axis=0, keepdims=True)
    every = jnp.sum(tallies.astype(jnp.float32), axis=1, keepdims=True)
    scale = 0.25 * jnp.sum(every, axis=0, keepdims=True) / K

    for d in range(1, subs):
        q = sub_after(d)
        cen_copy(q, q).wait_recv()

    @pl.loop(1, owners)
    def _(d):
        p = before(d)
        vec_copy(p, p).wait_recv()

    slab = arrived[...].astype(jnp.float32)
    full = jnp.concatenate(
        [
            slab[:, i * cap : (i + 1) * cap].reshape(rows, 128)
            for i in range(features // 128)
        ],
        axis=1,
    )
    packed = slab[:, features // 128 * cap :].reshape(owners * DS, 128)
    labels = jnp.concatenate(
        [
            jnp.broadcast_to(packed[:, i * 32 : i * 32 + 1], packed.shape).reshape(owners, DS, 128)
            for i in range(cap // DS)
        ],
        axis=1,
    ).reshape(rows, 128)
    lanes = lax.broadcasted_iota(jnp.int32, labels.shape, 1).astype(jnp.float32)
    selector = (labels == lanes).astype(jnp.float32).astype(jnp.bfloat16)
    lists = centres[...].reshape(subs * centres.shape[1], features)
    lists = jnp.concatenate(
        [lists, jnp.zeros((labels.shape[1] - lists.shape[0], features), lists.dtype)], axis=0
    )
    centre = jnp.dot(selector, lists, preferred_element_type=jnp.float32)
    residual = (full - centre).astype(jnp.bfloat16).astype(jnp.float32)
    res[...] = jnp.where(used > 0.0, residual.T, 0.0)

    def one_hot(t, m):
        return hot[t * spaces + m]

    def rows_of(m):
        return pl.ds(pl.multiple_of(m * DS, DS), DS)

    def part(p, t):
        sums = []
        tally = jnp.zeros((DS, K), jnp.float32)
        line = lax.broadcasted_iota(jnp.int32, (DS, K), 0)
        for j in range(pieces):
            m = p * pieces + j
            left = jnp.concatenate(
                [res[rows_of(m), :], jnp.broadcast_to(used, (DS, rows))], axis=0
            ).astype(jnp.bfloat16)
            both = lax.dot_general(
                left, one_hot(t, m), (((1,), (1,)), ((), ())),
                preferred_element_type=jnp.float32,
            )
            sums.append(both[:DS])
            number = both[DS:]
            coarse_part = jnp.floor(number * (1.0 / 128.0)) * 128.0
            tally = jnp.where(line == j, coarse_part, tally)
            tally = jnp.where(line == pieces + j, number - coarse_part, tally)
        return jnp.concatenate(sums + [tally], axis=0)

    def compute(d):
        c = chip_after(d)
        for t in range(ITERS):
            pair_out[c, t] = part(c * 2 + 1 - core, t).astype(jnp.bfloat16)
        pair_copy(c).start()
        for t in range(ITERS):
            kept[c, t] = part(c * 2 + core, t)

    compute(jnp.int32(1))

    @pl.loop(2, chips + 1)
    def _(d):
        compute(d)
        c = chip_after(d - 1)
        pair_copy(c).wait_recv()
        for t in range(ITERS):
            both = kept[c, t] + pair_in[c, t].astype(jnp.float32)
            parts_out[c, t] = both.astype(jnp.bfloat16)
        part_copy(c, chip).start()

    pair_copy(chip).wait_recv()
    for t in range(ITERS):
        total[t] = kept[chip, t] + pair_in[chip, t].astype(jnp.float32)

    @pl.loop(1, chips)
    def _(d):
        c = lax.rem(chip + chips - spread(d, chips), chips)
        part_copy(c, c).wait_recv()
        for t in range(ITERS):
            total[t] += parts_in[c, t].astype(jnp.float32)

    loads[3].wait()
    mine = []
    for j in range(pieces):
        book = init[rows_of(me * pieces + j), :]
        for t in range(ITERS):
            number = (
                total[t, height + j : height + j + 1]
                + total[t, height + pieces + j : height + pieces + j + 1]
            )
            book = (total[t, j * DS : (j + 1) * DS] + scale * book) / (number + scale)
        mine.append(book)
    mine = jnp.concatenate(mine, axis=0)
    books[me] = jnp.concatenate([mine[:, : K // 2], mine[:, K // 2 :]], axis=0).astype(
        jnp.bfloat16
    )

    @pl.loop(1, owners)
    def _(d):
        book_copy(after(d), me).start()

    def finish(p):
        pair = books[p].astype(jnp.float32)
        book = jnp.concatenate([pair[:height], pair[height:]], axis=1)
        for j in range(pieces):
            m = p * pieces + j
            own = book[j * DS : (j + 1) * DS]
            init[rows_of(m), :] = own
            picked = jnp.dot(
                own.astype(jnp.bfloat16), one_hot(ITERS - 1, m),
                preferred_element_type=jnp.float32,
            )
            res[rows_of(m), :] = jnp.where(used > 0.0, res[rows_of(m), :] - picked, 0.0)

    finish(me)

    @pl.loop(1, owners)
    def _(d):
        p = before(d)
        book_copy(p, p).wait_recv()
        finish(p)

    book_out[...] = init[...].astype(jnp.bfloat16)
    left_out[...] = res[...].astype(jnp.bfloat16)

    for d in range(1, subs):
        cen_copy(sub_after(d), my_sub).wait_send()

    @pl.loop(1, owners)
    def _(d):
        p = after(d)
        vec_copy(p, me).wait_send()
        book_copy(p, me).wait_send()

    @pl.loop(1, chips)
    def _(d):
        part_copy(chip_after(d), chip).wait_send()

    @pl.loop(0, chips)
    def _(c):
        pair_copy(c).wait_send()


def fused(vectors, list_ids, counts, coarse, codebook_init, codes):
    features, rows = vectors.shape
    owners = lax.axis_size("lists")
    subs = lax.axis_size("sub")
    cap = rows // owners
    height = features // owners
    vec = (owners, features // 128 * cap + DS, 128)
    slabs = (subs, coarse.shape[1], features)
    vmem = pl.BlockSpec(memory_space=pltpu.VMEM)
    hbm = pl.BlockSpec(memory_space=pl.ANY)
    dma = pltpu.SemaphoreType.DMA
    part = (owners // 2, ITERS, height + DS, K)
    codebook, leftover = pl.pallas_call(
        functools.partial(kernel, owners, subs),
        out_shape=(
            jax.ShapeDtypeStruct((features, K), jnp.bfloat16),
            jax.ShapeDtypeStruct((features, rows), jnp.bfloat16),
        ),
        in_specs=[hbm, vmem, vmem, hbm, hbm, hbm],
        out_specs=(vmem, vmem),
        scratch_shapes=[
            pltpu.VMEM(vectors.shape, jnp.bfloat16),
            pltpu.VMEM(coarse.shape[::-1], jnp.bfloat16),
            pltpu.VMEM(codes.shape, jnp.int32),
            pltpu.VMEM(vec, jnp.bfloat16),
            pltpu.VMEM(slabs, jnp.bfloat16),
            pltpu.VMEM((features, K), jnp.float32),
            pltpu.VMEM((ITERS * features // DS, K, rows), jnp.bfloat16),
            pltpu.VMEM(vec, jnp.bfloat16),
            pltpu.VMEM(slabs, jnp.bfloat16),
            pltpu.VMEM((features, rows), jnp.float32),
            pltpu.VMEM(part, jnp.bfloat16),
            pltpu.VMEM(part, jnp.bfloat16),
            pltpu.VMEM(part, jnp.float32),
            pltpu.VMEM(part, jnp.bfloat16),
            pltpu.VMEM(part, jnp.bfloat16),
            pltpu.VMEM(part[1:], jnp.float32),
            pltpu.VMEM((owners, 2 * height, K // 2), jnp.bfloat16),
            dma((owners,)), dma((owners,)), dma((subs,)), dma((subs,)),
            dma((owners // 2,)), dma((owners // 2,)), dma((owners,)), dma((owners,)),
            dma((owners // 2,)), dma((owners // 2,)), dma((4,)),
        ],
        compiler_params=pltpu.CompilerParams(
            collective_id=0, has_side_effects=True, vmem_limit_bytes=60 * 1024 * 1024
        ),
    )(vectors, list_ids, counts, coarse.T, codebook_init, codes)
    return (codebook.astype(jnp.float32), leftover)


def fits(owners, subs, vectors, coarse):
    features = vectors.shape[0] // subs
    rows = vectors.shape[1] // owners
    spaces = features // DS
    per = coarse.shape[1] // (owners * subs)
    return (
        features % 128 == 0
        and owners % 2 == 0
        and rows // owners <= 32
        and (features // 128 * (rows // owners) + DS) % 16 == 0
        and spaces % owners == 0
        and 2 * (spaces // owners) <= DS
        and (features // owners + DS) % 16 == 0
        and (rows // owners) % DS == 0
        and per % 16 == 0
        and per * subs <= 128
    )


def dispatch(owners, subs, *args):
    whole_features = args[0].shape[0] * subs
    sizes = (
        jax.ShapeDtypeStruct((whole_features, args[0].shape[1] * owners), jnp.bfloat16),
        jax.ShapeDtypeStruct((whole_features, args[3].shape[1] * owners * subs), jnp.bfloat16),
    )
    return (fused if fits(owners, subs, *sizes) else shards)(*args)


def solution(mesh):
    return jax.shard_map(
        functools.partial(dispatch, mesh.shape["lists"], mesh.shape["sub"]),
        mesh=mesh,
        in_specs=(
            P("sub", "lists"),
            P("lists"),
            P(),
            P(None, ("lists", "sub")),
            P("sub", None),
            P(None, "sub", "lists"),
        ),
        out_specs=(P("sub", None), P("sub", "lists")),
        check_vma=False,
    )
```

```python
import functools

import jax
import jax.numpy as jnp
from jax import lax
from jax.experimental import pallas as pl
from jax.experimental.pallas import tpu as pltpu
from jax.sharding import PartitionSpec as P

K = 256
DS = 8
LISTS_DEV = 64
ITERS = 2


def shards(vectors, list_ids, counts, coarse, codebook_init, codes):
    features, rows = vectors.shape
    owners = lax.axis_size("lists")
    owner = lax.axis_index("lists")
    block = rows // owners
    subspaces = features // DS
    mine = lax.all_to_all(coarse, "sub", split_axis=0, concat_axis=1, tiled=True)
    list_iota = jnp.arange(LISTS_DEV, dtype=jnp.int32)
    arrived = lax.all_to_all(vectors, "lists", split_axis=1, concat_axis=1, tiled=True)
    labels = lax.all_to_all(
        list_ids.reshape(1, rows), "lists", split_axis=1, concat_axis=1, tiled=True
    ).reshape(rows)
    selector = (labels[None, :] == list_iota[:, None]).astype(jnp.bfloat16)
    centre = jnp.dot(mine, selector, preferred_element_type=jnp.float32)
    residual = (arrived.astype(jnp.float32) - centre).astype(jnp.bfloat16)
    block_counts = lax.dynamic_index_in_dim(counts, owner, 1, keepdims=False)
    valid = (jnp.arange(block, dtype=jnp.int32)[None, :] < block_counts[:, None]).reshape(rows)
    code_iota = jnp.arange(K, dtype=jnp.int32)
    split_res = residual.reshape(subspaces, DS, rows)
    group_size = 4
    groups = subspaces // group_size
    grouped_res = split_res.reshape(groups, group_size, DS, rows)
    grouped_codes = jnp.swapaxes(codes, 0, 1).reshape(groups, group_size, ITERS, rows)

    def group_sums(packed):
        sub_res, sub_codes = packed
        one_hot = (sub_codes[:, :, None, :] == code_iota[None, None, :, None]) & valid[
            None, None, None, :
        ]
        one_hot = one_hot.astype(jnp.bfloat16)
        sums = jnp.einsum("gdr,gtkr->tgdk", sub_res, one_hot, preferred_element_type=jnp.float32)
        tally = jnp.swapaxes(jnp.sum(one_hot, axis=3, dtype=jnp.float32), 0, 1)
        return (sums, tally)

    part_sums, part_counts = lax.map(group_sums, (grouped_res, grouped_codes))
    part_sums = jnp.swapaxes(part_sums, 0, 1).reshape(ITERS, features, K)
    part_counts = jnp.swapaxes(part_counts, 0, 1).reshape(ITERS, subspaces, K)
    weight = 0.25 * jnp.sum(counts).astype(jnp.float32) / K
    total_sums, total_counts = lax.psum((part_sums, part_counts), "lists")
    codebook = codebook_init
    for iteration in range(ITERS):
        spread = jnp.repeat(total_counts[iteration], DS, axis=0)
        codebook = (total_sums[iteration] + weight * codebook) / (spread + weight)
    high = codebook.astype(jnp.bfloat16)
    low = (codebook - high.astype(jnp.float32)).astype(jnp.bfloat16)
    books = jnp.concatenate(
        [high.reshape(subspaces, DS, K), low.reshape(subspaces, DS, K)], axis=1
    ).reshape(groups, group_size, 2 * DS, K)

    def group_pick(packed):
        book, sub_codes = packed
        one_hot = (sub_codes[:, None, :] == code_iota[None, :, None]).astype(jnp.bfloat16)
        both = jnp.einsum("gdk,gkr->gdr", book, one_hot, preferred_element_type=jnp.float32)
        return both[:, :DS] + both[:, DS:]

    picked = lax.map(group_pick, (books, grouped_codes[:, :, ITERS - 1]))
    picked = picked.reshape(subspaces, DS, rows)
    leftover = jnp.where(valid[None, None, :], split_res.astype(jnp.float32) - picked, 0.0)
    leftover = leftover.astype(jnp.bfloat16).reshape(features, rows)
    return (codebook, leftover)


def remote(src, dst, send_sem, recv_sem, device):
    return pltpu.make_async_remote_copy(
        src_ref=src,
        dst_ref=dst,
        send_sem=send_sem,
        recv_sem=recv_sem,
        device_id=device,
        device_id_type=pl.DeviceIdType.MESH,
    )


def kernel(
    owners, subs, vectors_hbm, list_ids, counts, coarse_hbm, init_hbm, codes_hbm,
    book_out, left_out,
    vectors, own_coarse, codes,
    vec, coarse, init, hot, arrived, centres, res, pair_out, pair_in, kept, parts_out, parts_in,
    total, books,
    vec_send, vec_recv, cen_send, cen_recv, part_send, part_recv, book_send, book_recv,
    pair_send, pair_recv, load_sem,
):
    me = lax.axis_index("lists")
    my_sub = lax.axis_index("sub")
    features, rows = res.shape
    cap = rows // owners
    chips = owners // 2
    core = lax.rem(me, 2)
    chip = me // 2
    partner = chip * 2 + 1 - core
    spaces = features // DS
    pieces = features // DS // owners
    height = pieces * DS

    def after(d):
        return lax.rem(me + d, owners)

    def before(d):
        return lax.rem(me + owners - d, owners)

    def sub_after(d):
        return lax.rem(my_sub + d, subs)

    loads = [
        pltpu.make_async_copy(src, dst, load_sem.at[i])
        for i, (src, dst) in enumerate(
            ((vectors_hbm, vectors), (coarse_hbm, own_coarse), (codes_hbm, codes), (init_hbm, init))
        )
    ]
    for load in loads:
        load.start()

    barrier = pltpu.get_barrier_semaphore()

    @pl.loop(1, owners)
    def _(d):
        pl.semaphore_signal(
            barrier, inc=1, device_id={"lists": after(d)}, device_id_type=pl.DeviceIdType.MESH
        )

    for d in range(1, subs):
        pl.semaphore_signal(
            barrier, inc=1, device_id={"sub": sub_after(d)}, device_id_type=pl.DeviceIdType.MESH
        )
    loads[0].wait()
    loads[1].wait()
    for q in range(subs):
        coarse[q] = own_coarse[:, q * features : (q + 1) * features]
    tail = jnp.broadcast_to(list_ids[...].reshape(1, rows).astype(jnp.float32), (128, rows))
    slots = jnp.concatenate([vectors[...].astype(jnp.float32), tail], axis=0).T
    group = lax.broadcasted_iota(jnp.int32, (DS, 128), 1) // 32
    for s in range(owners):
        slot = slots[s * cap : (s + 1) * cap]
        label = jnp.zeros((DS, 128), jnp.float32)
        for i in range(cap // DS):
            label = jnp.where(group == i, slot[i * DS : (i + 1) * DS, features:], label)
        pack = [slot[:, c : c + 128] for c in range(0, features, 128)] + [label]
        vec[s] = jnp.concatenate(pack, axis=0).astype(jnp.bfloat16)
    pl.semaphore_wait(barrier, owners - 1 + subs - 1)

    def cen_copy(q, slot):
        return remote(
            coarse.at[q], centres.at[slot], cen_send.at[q], cen_recv.at[slot], {"sub": q}
        )

    def vec_copy(p, slot):
        return remote(
            vec.at[p], arrived.at[slot], vec_send.at[p], vec_recv.at[slot], {"lists": p}
        )

    def pair_copy(c):
        return remote(
            pair_out.at[c], pair_in.at[c], pair_send.at[c], pair_recv.at[c], {"lists": partner}
        )

    def part_copy(c, slot):
        return remote(
            parts_out.at[c], parts_in.at[slot], part_send.at[c], part_recv.at[slot],
            {"lists": c * 2 + core},
        )

    def chip_after(d):
        return lax.rem(chip + d, chips)

    def book_copy(p, slot):
        return remote(
            books.at[me], books.at[slot], book_send.at[p], book_recv.at[slot], {"lists": p}
        )

    for d in range(1, subs):
        cen_copy(sub_after(d), my_sub).start()

    @pl.loop(1, owners)
    def _(d):
        vec_copy(after(d), me).start()

    arrived[me] = vec[me]
    centres[my_sub] = coarse[my_sub]
    loads[2].wait()
    iota = lax.broadcasted_iota(jnp.int32, (16, rows), 0).astype(jnp.float32)

    @pl.loop(0, spaces)
    def _(m):
        for t in range(ITERS):
            code = codes[t, pl.ds(m, 1), :].astype(jnp.float32)
            code = jnp.broadcast_to(code, (16, rows)).astype(jnp.bfloat16)
            for k in range(0, K, 16):
                same = code == (iota + k).astype(jnp.bfloat16)
                hot[t * spaces + m, k : k + 16, :] = jnp.where(
                    same, jnp.ones_like(code), jnp.zeros_like(code)
                )

    tallies = counts[...]
    line = lax.broadcasted_iota(jnp.int32, tallies.shape, 1)
    senders = jnp.sum(
        jnp.where(line == me, tallies, 0).astype(jnp.float32), axis=1, keepdims=True
    )
    first = lax.broadcasted_iota(jnp.int32, (owners, rows), 0) * cap
    place = (lax.broadcasted_iota(jnp.int32, (owners, rows), 1) - first).astype(jnp.float32)
    inside = jnp.where(place >= 0.0, 1.0, 0.0) * jnp.where(place < senders, 1.0, 0.0)
    used = jnp.max(inside, axis=0, keepdims=True)
    every = jnp.sum(tallies.astype(jnp.float32), axis=1, keepdims=True)
    scale = 0.25 * jnp.sum(every, axis=0, keepdims=True) / K

    for d in range(1, subs):
        q = sub_after(d)
        cen_copy(q, q).wait_recv()

    @pl.loop(1, owners)
    def _(d):
        p = before(d)
        vec_copy(p, p).wait_recv()

    slab = arrived[...].astype(jnp.float32)
    full = jnp.concatenate(
        [
            slab[:, i * cap : (i + 1) * cap].reshape(rows, 128)
            for i in range(features // 128)
        ],
        axis=1,
    )
    packed = slab[:, features // 128 * cap :].reshape(owners * DS, 128)
    labels = jnp.concatenate(
        [
            jnp.broadcast_to(packed[:, i * 32 : i * 32 + 1], packed.shape).reshape(owners, DS, 128)
            for i in range(cap // DS)
        ],
        axis=1,
    ).reshape(rows, 128)
    lanes = lax.broadcasted_iota(jnp.int32, labels.shape, 1).astype(jnp.float32)
    selector = (labels == lanes).astype(jnp.float32).astype(jnp.bfloat16)
    lists = centres[...].reshape(subs * centres.shape[1], features)
    lists = jnp.concatenate(
        [lists, jnp.zeros((labels.shape[1] - lists.shape[0], features), lists.dtype)], axis=0
    )
    centre = jnp.dot(selector, lists, preferred_element_type=jnp.float32)
    residual = (full - centre).astype(jnp.bfloat16).astype(jnp.float32)
    res[...] = jnp.where(used > 0.0, residual.T, 0.0)

    def one_hot(t, m):
        return hot[t * spaces + m]

    def rows_of(m):
        return pl.ds(pl.multiple_of(m * DS, DS), DS)

    def part(p, t):
        sums = []
        tally = jnp.zeros((DS, K), jnp.float32)
        line = lax.broadcasted_iota(jnp.int32, (DS, K), 0)
        for j in range(pieces):
            m = p * pieces + j
            left = jnp.concatenate(
                [res[rows_of(m), :], jnp.broadcast_to(used, (DS, rows))], axis=0
            ).astype(jnp.bfloat16)
            both = lax.dot_general(
                left, one_hot(t, m), (((1,), (1,)), ((), ())),
                preferred_element_type=jnp.float32,
            )
            sums.append(both[:DS])
            number = both[DS:]
            coarse_part = jnp.floor(number * (1.0 / 128.0)) * 128.0
            tally = jnp.where(line == j, coarse_part, tally)
            tally = jnp.where(line == pieces + j, number - coarse_part, tally)
        return jnp.concatenate(sums + [tally], axis=0)

    def compute(d):
        c = chip_after(d)
        for t in range(ITERS):
            pair_out[c, t] = part(c * 2 + 1 - core, t).astype(jnp.bfloat16)
        pair_copy(c).start()
        for t in range(ITERS):
            kept[c, t] = part(c * 2 + core, t)

    compute(1)

    @pl.loop(2, chips + 1)
    def _(d):
        compute(d)
        c = chip_after(d - 1)
        pair_copy(c).wait_recv()
        for t in range(ITERS):
            both = kept[c, t] + pair_in[c, t].astype(jnp.float32)
            parts_out[c, t] = both.astype(jnp.bfloat16)
        part_copy(c, chip).start()

    pair_copy(chip).wait_recv()
    for t in range(ITERS):
        total[t] = kept[chip, t] + pair_in[chip, t].astype(jnp.float32)

    @pl.loop(1, chips)
    def _(d):
        c = lax.rem(chip + chips - d, chips)
        part_copy(c, c).wait_recv()
        for t in range(ITERS):
            total[t] += parts_in[c, t].astype(jnp.float32)

    loads[3].wait()
    mine = []
    for j in range(pieces):
        book = init[rows_of(me * pieces + j), :]
        for t in range(ITERS):
            number = (
                total[t, height + j : height + j + 1]
                + total[t, height + pieces + j : height + pieces + j + 1]
            )
            book = (total[t, j * DS : (j + 1) * DS] + scale * book) / (number + scale)
        mine.append(book)
    mine = jnp.concatenate(mine, axis=0)
    books[me] = jnp.concatenate([mine[:, : K // 2], mine[:, K // 2 :]], axis=0).astype(
        jnp.bfloat16
    )

    @pl.loop(1, owners)
    def _(d):
        book_copy(after(d), me).start()

    def finish(senders):
        stores = []
        for p in senders:
            pair = books[p].astype(jnp.float32)
            book = jnp.concatenate([pair[:height], pair[height:]], axis=1)
            for j in range(pieces):
                m = p * pieces + j
                own = book[j * DS : (j + 1) * DS]
                picked = jnp.dot(
                    own.astype(jnp.bfloat16), one_hot(ITERS - 1, m),
                    preferred_element_type=jnp.float32,
                )
                left = jnp.where(used > 0.0, res[rows_of(m), :] - picked, 0.0)
                stores.append((m, own, left))
        for m, own, left in stores:
            init[rows_of(m), :] = own
            res[rows_of(m), :] = left

    finish([me])
    batch = 3 if (owners - 1) % 3 == 0 else 1

    @pl.loop(0, (owners - 1) // batch)
    def _(i):
        senders = [before(i * batch + 1 + e) for e in range(batch)]
        for p in senders:
            book_copy(p, p).wait_recv()
        finish(senders)

    book_out[...] = init[...].astype(jnp.bfloat16)
    left_out[...] = res[...].astype(jnp.bfloat16)

    for d in range(1, subs):
        cen_copy(sub_after(d), my_sub).wait_send()

    @pl.loop(1, owners)
    def _(d):
        p = after(d)
        vec_copy(p, me).wait_send()
        book_copy(p, me).wait_send()

    @pl.loop(1, chips)
    def _(d):
        part_copy(chip_after(d), chip).wait_send()

    @pl.loop(0, chips)
    def _(c):
        pair_copy(c).wait_send()


def fused(vectors, list_ids, counts, coarse, codebook_init, codes):
    features, rows = vectors.shape
    owners = lax.axis_size("lists")
    subs = lax.axis_size("sub")
    cap = rows // owners
    height = features // owners
    vec = (owners, features // 128 * cap + DS, 128)
    slabs = (subs, coarse.shape[1], features)
    vmem = pl.BlockSpec(memory_space=pltpu.VMEM)
    hbm = pl.BlockSpec(memory_space=pl.ANY)
    dma = pltpu.SemaphoreType.DMA
    part = (owners // 2, ITERS, height + DS, K)
    codebook, leftover = pl.pallas_call(
        functools.partial(kernel, owners, subs),
        out_shape=(
            jax.ShapeDtypeStruct((features, K), jnp.bfloat16),
            jax.ShapeDtypeStruct((features, rows), jnp.bfloat16),
        ),
        in_specs=[hbm, vmem, vmem, hbm, hbm, hbm],
        out_specs=(vmem, vmem),
        scratch_shapes=[
            pltpu.VMEM(vectors.shape, jnp.bfloat16),
            pltpu.VMEM(coarse.shape[::-1], jnp.bfloat16),
            pltpu.VMEM(codes.shape, jnp.int32),
            pltpu.VMEM(vec, jnp.bfloat16),
            pltpu.VMEM(slabs, jnp.bfloat16),
            pltpu.VMEM((features, K), jnp.float32),
            pltpu.VMEM((ITERS * features // DS, K, rows), jnp.bfloat16),
            pltpu.VMEM(vec, jnp.bfloat16),
            pltpu.VMEM(slabs, jnp.bfloat16),
            pltpu.VMEM((features, rows), jnp.float32),
            pltpu.VMEM(part, jnp.bfloat16),
            pltpu.VMEM(part, jnp.bfloat16),
            pltpu.VMEM(part, jnp.float32),
            pltpu.VMEM(part, jnp.bfloat16),
            pltpu.VMEM(part, jnp.bfloat16),
            pltpu.VMEM(part[1:], jnp.float32),
            pltpu.VMEM((owners, 2 * height, K // 2), jnp.bfloat16),
            dma((owners,)), dma((owners,)), dma((subs,)), dma((subs,)),
            dma((owners // 2,)), dma((owners // 2,)), dma((owners,)), dma((owners,)),
            dma((owners // 2,)), dma((owners // 2,)), dma((4,)),
        ],
        compiler_params=pltpu.CompilerParams(
            collective_id=0, has_side_effects=True, vmem_limit_bytes=60 * 1024 * 1024
        ),
    )(vectors, list_ids, counts, coarse.T, codebook_init, codes)
    return (codebook.astype(jnp.float32), leftover)


def fits(owners, subs, vectors, coarse):
    features = vectors.shape[0] // subs
    rows = vectors.shape[1] // owners
    spaces = features // DS
    per = coarse.shape[1] // (owners * subs)
    return (
        features % 128 == 0
        and owners % 2 == 0
        and rows // owners <= 32
        and (features // 128 * (rows // owners) + DS) % 16 == 0
        and spaces % owners == 0
        and 2 * (spaces // owners) <= DS
        and (features // owners + DS) % 16 == 0
        and (rows // owners) % DS == 0
        and per % 16 == 0
        and per * subs <= 128
    )


def dispatch(owners, subs, *args):
    whole_features = args[0].shape[0] * subs
    sizes = (
        jax.ShapeDtypeStruct((whole_features, args[0].shape[1] * owners), jnp.bfloat16),
        jax.ShapeDtypeStruct((whole_features, args[3].shape[1] * owners * subs), jnp.bfloat16),
    )
    return (fused if fits(owners, subs, *sizes) else shards)(*args)


def solution(mesh):
    return jax.shard_map(
        functools.partial(dispatch, mesh.shape["lists"], mesh.shape["sub"]),
        mesh=mesh,
        in_specs=(
            P("sub", "lists"),
            P("lists"),
            P(),
            P(None, ("lists", "sub")),
            P("sub", None),
            P(None, "sub", "lists"),
        ),
        out_specs=(P("sub", None), P("sub", "lists")),
        check_vma=False,
    )
```
